512 devices in a mesh: walk: 32 (over z_hi, y), chol: 16 (over z_lo, x, core).
Axes of the slice: x: 4, y: 8, z: 8 (z_hi: 4, z_lo: 2; z = z_hi * 2 + z_lo), core: 2. Of those that a mesh axis runs over, the one named last changes fastest.
Arguments:
- cholesky: bfloat16 [32, 1024, 1024], P('chol'), may hold values from -0.1875 to 0.1875
- half_rotated: bfloat16 [32, 100, 1024], P('chol'), may hold values from -0.09375 to 0.09375
- green_half: bfloat16 [256, 100, 1024], P('walk', None, 'chol'), may hold values from -6 to 6
- walker: bfloat16 [256, 100, 1024], P('walk', None, 'chol'), may hold values from -6 to 6
- aux_noise: float32 [256, 32], P('walk', 'chol'), may hold values from -6 to 6
- mf_shift: float32 [4000], replicated, may hold values from -30 to 30
- chol_index: int32 [32], P('chol'), may hold values from 0 to 3999, as said below
- walker_source: int32 [256], P('walk'), may hold values from 0 to 255, each once
Outputs:
- moved_walker: bfloat16 [256, 100, 1024], P('walk', None, 'chol')
The draws below stay inside these ranges and needn't reach their ends.
Inputs may be any that keep to these rules, and one draw needn't show every extreme that they name: `chol_index`: the 32 entries are distinct; both 0 and 3999 occur. `walker_source`: each walker is named by exactly one slot.
All inputs are finite; a program needn't handle non-finite values.
Results may differ from the reference program's by a relative error of at most 0.02.
Values may be sent and summed in bfloat16 or wider, within the bound.
A program may use at most 64 MiB of HBM per device.

```python
import jax
import jax.numpy as jnp
from jax import lax

NORB = 1024
NOCC = 100
NCHOL_ALL = 4000
CHOL_DEV = 2
NWIN = 32
WALKERS = 256
N_CHOL = 16


def draw_chol_index(key, part):
    key = jax.random.fold_in(key, 7)
    middle = jax.random.permutation(key, NCHOL_ALL - 2).astype(jnp.int32) + 1
    ends = jnp.array([0, NCHOL_ALL - 1], jnp.int32)
    picked = jnp.concatenate([ends, middle[:NWIN - 2]])
    return jax.random.permutation(jax.random.fold_in(key, 1), picked)


def block_scale(own_key, extent, split, smallest, high):
    loudness, own = 1.0, jax.random.fold_in(own_key, 6)
    for position, shards_of in split:
        steps = jnp.exp(jax.random.uniform(jax.random.fold_in(own, position), (shards_of,), jnp.float32, smallest / len(split), high / len(split)))
        loudness = loudness * jnp.repeat(steps, extent[position] // shards_of).reshape([-1 if axis == position else 1 for axis in range(len(extent))])
    return loudness


def bell_draw(rng, dims, width, bound, pieces=(), kind=jnp.bfloat16):
    gain = block_scale(rng, dims, pieces, -0.22, 0.18) if pieces else 1.0
    result = jax.random.normal(rng, dims, jnp.float32) * width * gain
    return jnp.minimum(jnp.maximum(result, -bound), bound).astype(kind)


def setup_inputs(seed: int = 0) -> dict:
    splits = jax.random.split(jax.random.key(seed), 9)
    return {
        "cholesky": bell_draw(splits[0], (NWIN, NORB, NORB), NORB ** -0.5, 0.1875, ((0, 16),)),
        "half_rotated": bell_draw(splits[1], (NWIN, NOCC, NORB), (NOCC * NORB // 25) ** -0.5, 0.09375, ((0, 16),)),
        "green_half": bell_draw(splits[2], (WALKERS, NOCC, NORB), 1.0, 6.0, ((0, 32), (2, 16))),
        "walker": bell_draw(splits[3], (WALKERS, NOCC, NORB), 1.0, 6.0, ((0, 32), (2, 16))),
        "aux_noise": bell_draw(splits[4], (WALKERS, NWIN), 1.0, 6.0, ((0, 32), (1, 16)), jnp.float32),
        "mf_shift": bell_draw(splits[5], (NCHOL_ALL,), 5.0, 30.0, (), jnp.float32),
        "chol_index": draw_chol_index(jax.random.fold_in(splits[8], 71), 0),
        "walker_source": jax.random.permutation(splits[7], WALKERS).astype(jnp.int32),
    }


field_scale = 0.1


def block_apply(source, aux_field, cholesky):
    flat_rows = source.astype(jnp.float32).reshape(WALKERS * NOCC, NORB)
    blocks = cholesky.reshape(N_CHOL, CHOL_DEV, NORB, NORB)
    coeff_blocks = aux_field.reshape(WALKERS, N_CHOL, CHOL_DEV).transpose(1, 2, 0)

    def one_block(carried, pair):
        matrices, coeffs = pair
        partial_value = jnp.zeros((WALKERS, NOCC, NORB), jnp.float32)
        for vector in range(CHOL_DEV):
            product = lax.dot_general(flat_rows, matrices[vector].astype(jnp.float32),
                                      (((1,), (1,)), ((), ())), precision=lax.Precision.HIGHEST)
            partial_value = partial_value + coeffs[vector][:, None, None] * product.reshape(WALKERS, NOCC, NORB)
        rounded = lax.optimization_barrier(partial_value.astype(jnp.bfloat16)).astype(jnp.float32)
        return carried + rounded, None

    summed, _ = lax.scan(one_block, jnp.zeros((WALKERS, NOCC, NORB), jnp.float32), (blocks, coeff_blocks))
    return summed


def reference(cholesky, half_rotated, green_half, walker, aux_noise, mf_shift, chol_index, walker_source):
    shift_mean = mf_shift[chol_index]
    bias_sum = jnp.einsum("wik,gik->wg", green_half.astype(jnp.float32), half_rotated.astype(jnp.float32),
                          precision=lax.Precision.HIGHEST)
    aux_field = aux_noise + field_scale * (bias_sum - shift_mean[None, :])
    first_sum = block_apply(walker, aux_field, cholesky)
    first_term = field_scale * first_sum
    first_round = lax.optimization_barrier(first_term.astype(jnp.bfloat16))
    second_sum = block_apply(first_round, aux_field, cholesky)
    propagated = (walker.astype(jnp.float32) + first_term + 0.5 * field_scale * second_sum).astype(jnp.bfloat16)
    return jnp.take(propagated, walker_source, axis=0)
```

```python
import jax
import jax.numpy as jnp
from jax import lax
from jax.experimental import pallas as pl
from jax.experimental.pallas import tpu as pltpu
from jax.sharding import PartitionSpec as P

MESH = pl.DeviceIdType.MESH
field_scale = 0.1
CHUNKS = 4
TILES = 8
WALK = 32


def body(
    chol_ref, half_ref, green_ref, walker_ref, noise_ref, mean_ref, index_ref, source_ref,
    out_ref,
    lst, xg1, xg2, part, hop1, hop2, hopz_src, hopz, first, acc, hrg, gp, fb, btile, final,
    zsend, zrecv, ysend, yrecv, stile, sall,
    ag_s, ag_r, rs_s, rs_r, hr_s, hr_r, b_s, b_r, w_s, w_r, z_s, z_r, y_s, y_r, misc,
):
    walk = lax.axis_index("walk")
    chol = lax.axis_index("chol")
    core = chol % 2
    chip = chol // 2
    x, z = chip % 4, chip // 4
    xn, xp, xf, zo = (x + 1) % 4, (x + 3) % 4, (x + 2) % 4, 1 - z

    def at(zz, xx, cc):
        return zz * 8 + xx * 2 + cc

    dev_z = {"chol": at(zo, x, core)}
    dev_n = {"chol": at(z, xn, core)}
    dev_p = {"chol": at(z, xp, core)}
    dev_sib = {"chol": at(z, x, 1 - core)}

    own_l = pltpu.make_async_copy(
        chol_ref.at[:, :, core], lst.at[pl.ds(2 * core, 2)], misc.at[0]
    )
    own_l.start()
    own_h = pltpu.make_async_copy(
        half_ref.at[:, :, pl.ds(pl.multiple_of(chip * 128, 128), 128)],
        hrg.at[chip, :, pl.ds(0, 112)],
        misc.at[1],
    )
    own_h.start()

    barrier = pltpu.get_barrier_semaphore()

    @pl.loop(1, 16)
    def _(d):
        pl.semaphore_signal(
            barrier, inc=1, device_id={"chol": (chol + d) % 16}, device_id_type=MESH
        )

    @pl.loop(1, WALK)
    def _(d):
        pl.semaphore_signal(
            barrier, inc=1, device_id={"walk": (walk + d) % WALK}, device_id_type=MESH
        )

    gp[:, core] = jnp.zeros((8, 64, 128), jnp.bfloat16)
    gp[:, core, :, 0:100] = green_ref[...]
    xg1[:, chol] = jnp.zeros((TILES, 64, 128), jnp.bfloat16)
    xg1[:, chol, :, 0:100] = walker_ref[...]
    hrg[:, :, 112:128, :] = jnp.zeros((8, 2, 16, 128), jnp.bfloat16)

    row8 = lax.broadcasted_iota(jnp.int32, (8, 128), 0)
    lane8 = lax.broadcasted_iota(jnp.int32, (8, 128), 1)
    ids = jnp.zeros((8, 128), jnp.int32)
    for s in range(8):
        value = source_ref[s]
        ids = jnp.where(row8 == s, (value // 8) * 16 + value % 8, ids)
    stile[...] = ids
    sall[walk] = ids

    pl.semaphore_wait(barrier, 15 + WALK - 1)

    def remote(src, dst, ssem, rsem, dev):
        return pltpu.make_async_remote_copy(
            src_ref=src, dst_ref=dst, send_sem=ssem, recv_sem=rsem,
            device_id=dev, device_id_type=MESH,
        )

    g_copy = remote(gp.at[:, core], gp.at[:, core], misc.at[2], misc.at[3], dev_sib)
    g_copy.start()
    g_got = remote(gp.at[:, 1 - core], gp.at[:, 1 - core], misc.at[2], misc.at[3], dev_sib)

    others = ((0, 1), (0, 3), (1, 0), (1, 1), (1, 3), (0, 2), (1, 2))

    def hr_copy(k, dz, dx):
        there = ((z + dz) % 2) * 4 + (x + dx) % 4
        return remote(
            half_ref.at[:, :, pl.ds(pl.multiple_of(there * 128, 128), 128)],
            hrg.at[chip, :, pl.ds(0, 112)],
            hr_s.at[k], hr_r.at[k], {"chol": there * 2 + core},
        )

    def hr_got(k, dz, dx):
        there = ((z + dz) % 2) * 4 + (x + 4 - dx) % 4
        return remote(
            hrg.at[there, :, pl.ds(0, 112)], hrg.at[there, :, pl.ds(0, 112)],
            hr_s.at[k], hr_r.at[k], dev_z,
        )

    for k, (dz, dx) in enumerate(others):
        hr_copy(k, dz, dx).start()

    l_copy = remote(
        chol_ref.at[:, :, 1 - core], lst.at[pl.ds(2 * core, 2)], misc.at[4], misc.at[5], dev_sib
    )
    l_got = remote(
        lst.at[pl.ds(2 * (1 - core), 2)], lst.at[pl.ds(2 * (1 - core), 2)],
        misc.at[4], misc.at[5], dev_sib,
    )

    def ag_parts(xg, j, kind, sending, cc):
        full, low, high = pl.ds(2 * j, 2), 2 * j, 2 * j + 1
        send = {
            0: (full, z, x), 1: (full, z, x), 2: (full, z, x),
            3: (full, zo, x), 4: (full, zo, x),
            5: (low, z, xp), 6: (high, z, xn), 7: (low, zo, xp), 8: (high, zo, xn),
        }
        recv = {
            0: (full, zo, x), 1: (full, z, xp), 2: (full, z, xn),
            3: (full, zo, xp), 4: (full, zo, xn),
            5: (low, z, xf), 6: (high, z, xf), 7: (low, zo, xf), 8: (high, zo, xf),
        }
        tiles, zz, xx = (send if sending else recv)[kind]
        return xg.at[tiles, at(zz, xx, cc)]

    def ag_dev(kind):
        return dev_z if kind == 0 else (dev_n if kind in (1, 3, 5, 7) else dev_p)

    def ag_send(ph, xg, j, kind):
        ref = ag_parts(xg, j, kind, True, core)
        return remote(ref, ref, ag_s.at[ph, j, kind], ag_r.at[ph, j, kind], ag_dev(kind))

    def ag_got(ph, xg, j, kind):
        ref = ag_parts(xg, j, kind, False, core)
        return remote(ref, ref, ag_s.at[ph, j, kind], ag_r.at[ph, j, kind], ag_dev(kind))

    def sib_part(xg, j, kind, cc):
        if kind == 9:
            return xg.at[pl.ds(2 * j, 2), at(z, x, cc)]
        return ag_parts(xg, j, kind - 10, False, cc)

    def sib(ph, xg, j, kind, cc):
        ref = sib_part(xg, j, kind, cc)
        return remote(ref, ref, ag_s.at[ph, j, kind], ag_r.at[ph, j, kind], dev_sib)

    def ag_start(ph, xg, j):
        for kind in (1, 2, 0):
            ag_send(ph, xg, j, kind).start()
        sib(ph, xg, j, 9, core).start()

    def ag_arrive(ph, xg, j, kind, onward):
        ag_got(ph, xg, j, kind).wait_recv()
        for k in onward:
            ag_send(ph, xg, j, k).start()
        sib(ph, xg, j, 10 + kind, core).start()

    def ag_fwd1(ph, xg, j):
        ag_arrive(ph, xg, j, 0, (3, 4))
        ag_arrive(ph, xg, j, 1, (5,))
        ag_arrive(ph, xg, j, 2, (6,))

    def ag_fwd2(ph, xg, j):
        ag_arrive(ph, xg, j, 3, (7,))
        ag_arrive(ph, xg, j, 4, (8,))

    def ag_fwd3(ph, xg, j):
        for kind in (5, 6, 7, 8):
            ag_arrive(ph, xg, j, kind, ())

    def ag_fin(ph, xg, j):
        for kind in range(9, 19):
            sib(ph, xg, j, kind, 1 - core).wait_recv()

    def rs_copy(ph, j, kind):
        if kind == 0:
            src, dst, dev = part.at[ph, j, :, xf, 0], hop1.at[ph, j, 0], dev_n
        elif kind == 1:
            src, dst, dev = part.at[ph, j, :, xf, 1], hop1.at[ph, j, 1], dev_p
        elif kind == 2:
            src, dst, dev = part.at[ph, j, :, xn], hop2.at[ph, j, 0], dev_n
        elif kind == 3:
            src, dst, dev = part.at[ph, j, :, xp], hop2.at[ph, j, 1], dev_p
        else:
            src, dst, dev = hopz_src.at[ph, j], hopz.at[ph, j], dev_z
        return remote(src, dst, rs_s.at[ph, j, kind], rs_r.at[ph, j, kind], dev)

    f32 = jnp.float32

    def rs_start(ph, j):
        rs_copy(ph, j, 0).start()
        rs_copy(ph, j, 1).start()

    def rs_mid(ph, j):
        for kind, where in ((0, xn), (1, xp)):
            rs_copy(ph, j, kind).wait_recv()
            part[ph, j, :, where, kind] = (
                part[ph, j, :, where, kind].astype(f32) + hop1[ph, j, kind].astype(f32)
            ).astype(jnp.bfloat16)
            rs_copy(ph, j, kind + 2).start()

    def summed(ph, j, zz):
        return (
            part[ph, j, zz, x].astype(f32)
            + hop2[ph, j, 0, zz].astype(f32)
            + hop2[ph, j, 1, zz].astype(f32)
        )

    def rs_last(ph, j):
        rs_copy(ph, j, 2).wait_recv()
        rs_copy(ph, j, 3).wait_recv()
        hopz_src[ph, j] = summed(ph, j, zo).astype(jnp.bfloat16)
        rs_copy(ph, j, 4).start()

    def rs_fin(ph, j):
        rs_copy(ph, j, 4).wait_recv()
        return summed(ph, j, z) + hopz[ph, j].astype(f32)

    def matmul(ph, xg, j):
        both = jnp.concatenate(
            [xg[2 * j].reshape(1024, 128), xg[2 * j + 1].reshape(1024, 128)], axis=1
        )
        for g in range(4):
            rows = lst[g].reshape(512, 1024)
            product = jnp.dot(rows, both, preferred_element_type=f32)
            scale = jnp.concatenate(
                [fb[g, pl.ds(2 * j, 1), :], fb[g, pl.ds(2 * j + 1, 1), :]], axis=1
            )
            if g == 0:
                acc[...] = product * scale
            else:
                acc[...] += product * scale
        for zz in range(2):
            for xx in range(4):
                for t in range(2):
                    part[ph, j, zz, xx, t] = acc[
                        pl.ds((zz * 4 + xx) * 64, 64), pl.ds(128 * t, 128)
                    ].astype(jnp.bfloat16)

    for j in range(CHUNKS):
        ag_start(0, xg1, j)
    l_copy.start()

    def s_copy(d, sending):
        there = (walk + d) % WALK if sending else (walk + WALK - d) % WALK
        return remote(
            stile, sall.at[walk] if sending else sall.at[there],
            w_s.at[d], w_r.at[d], {"walk": there},
        )

    @pl.loop(1, WALK)
    def _(d):
        s_copy(d, True).start()

    own_h.wait()
    g_got.wait_recv()
    for k, (dz, dx) in enumerate(others):
        hr_got(k, dz, dx).wait_recv()

    eye = (
        lax.broadcasted_iota(jnp.int32, (128, 128), 0)
        == lax.broadcasted_iota(jnp.int32, (128, 128), 1)
    ).astype(f32)
    greens = gp[...].reshape(1024, 128)

    def one_vector(v, tile):
        source, which = v // 2, v % 2
        product = jnp.dot(greens, hrg[source, which], preferred_element_type=f32)
        picked = jnp.sum(product.reshape(8, 128, 128) * eye[None], axis=1)
        value = jnp.sum(picked, axis=1, keepdims=True)
        return jnp.where(lane8 == source * 4 + core * 2 + which, field_scale * value, tile)

    tile = lax.fori_loop(0, 16, one_vector, jnp.zeros((8, 128), f32))
    for which in range(2):
        shift = mean_ref[index_ref[which]]
        for w in range(8):
            tile = tile + jnp.where(
                (row8 == w) & (lane8 == chol * 2 + which),
                noise_ref[which, w] - field_scale * shift, 0.0,
            )
    btile[chol] = tile

    def b_copy(d, sending):
        there = (chol + d) % 16 if sending else (chol + 16 - d) % 16
        slot = chol if sending else there
        return remote(
            btile.at[slot], btile.at[slot], b_s.at[d], b_r.at[d], {"chol": there}
        )

    @pl.loop(1, 16)
    def _(d):
        b_copy(d, True).start()

    for j in range(CHUNKS):
        ag_fwd1(0, xg1, j)
        if j >= 1:
            ag_fwd2(0, xg1, j - 1)
        if j >= 2:
            ag_fwd3(0, xg1, j - 2)
    ag_fwd2(0, xg1, CHUNKS - 1)
    ag_fwd3(0, xg1, CHUNKS - 2)

    @pl.loop(1, 16)
    def _(d):
        b_copy(d, False).wait_recv()

    field = btile[0]
    for c in range(1, 16):
        field = field + btile[c]
    for g in range(4):
        value = jnp.sum(
            jnp.where(lane8 == chip * 4 + g, field, 0.0), axis=1, keepdims=True
        )
        fb[g] = jnp.broadcast_to(value, (8, 128))

    own_l.wait()
    l_got.wait_recv()

    for t in range(CHUNKS + 9):
        def chunk(lag):
            return t - lag if 0 <= t - lag < CHUNKS else None

        j = chunk(9)
        if j is not None:
            second = rs_fin(1, j)
            moved = (
                xg1[pl.ds(2 * j, 2), chol].astype(f32)
                + first[pl.ds(2 * j, 2)]
                + (0.5 * field_scale) * second
            )
            final[pl.ds(128 * j, 128)] = moved.reshape(128, 128)
        j = chunk(8)
        if j is not None:
            rs_last(1, j)
        j = chunk(7)
        if j is not None:
            rs_mid(1, j)
        j = chunk(5)
        if j is not None:
            ag_fwd2(1, xg2, j)
        j = chunk(4)
        if j is not None:
            ag_fwd1(1, xg2, j)
        j = chunk(3)
        if j is not None:
            term = field_scale * rs_fin(0, j)
            first[pl.ds(2 * j, 2)] = term
            xg2[pl.ds(2 * j, 2), chol] = term.astype(jnp.bfloat16)
            ag_start(1, xg2, j)
        j = chunk(2)
        if j is not None:
            rs_last(0, j)
        j = chunk(1)
        if j is not None:
            rs_mid(0, j)
        j = chunk(0)
        if j is not None:
            if j == CHUNKS - 1:
                ag_fwd3(0, xg1, j)
            ag_fin(0, xg1, j)
            matmul(0, xg1, j)
            rs_start(0, j)
        j = chunk(6)
        if j is not None:
            ag_fwd3(1, xg2, j)
            ag_fin(1, xg2, j)
            matmul(1, xg2, j)
            rs_start(1, j)

    for p in range(WALK):
        zsend[p] = jnp.concatenate(
            [final[pl.ds(2 * p, 8, stride=64), :], final[pl.ds(2 * p + 1, 8, stride=64), :]],
            axis=0,
        ).astype(jnp.bfloat16)
    zrecv[walk] = zsend[walk]

    def z_copy(d, sending):
        there = (walk + d) % WALK if sending else (walk + WALK - d) % WALK
        return remote(
            zsend.at[there], zrecv.at[walk] if sending else zrecv.at[there],
            z_s.at[d], z_r.at[d], {"walk": there},
        )

    def y_copy(d, sending):
        there = (walk + d) % WALK if sending else (walk + WALK - d) % WALK
        return remote(
            ysend.at[there], yrecv.at[walk] if sending else yrecv.at[there],
            y_s.at[d], y_r.at[d], {"walk": there},
        )

    @pl.loop(1, WALK)
    def _(d):
        z_copy(d, True).start()

    @pl.loop(1, WALK)
    def _(d):
        s_copy(d, False).wait_recv()

    low = sall[...]
    wanted = jnp.stack([low, low + 8], axis=1).reshape(WALK * 16, 128)
    lanes = lax.broadcasted_iota(jnp.int32, (WALK * 16, 128), 1)
    picks = [
        jnp.where(wanted == lanes + 128 * b, 1.0, 0.0).astype(jnp.bfloat16) for b in range(4)
    ]

    @pl.loop(1, WALK)
    def _(d):
        z_copy(d, False).wait_recv()

    here = zrecv[...].reshape(WALK * 16, 128)
    taken = jnp.dot(picks[0], here[0:128], preferred_element_type=f32)
    for b in range(1, 4):
        taken = taken + jnp.dot(
            picks[b], here[128 * b : 128 * (b + 1)], preferred_element_type=f32
        )
    ysend[...] = taken.astype(jnp.bfloat16).reshape(WALK, 16, 128)
    yrecv[walk] = ysend[walk]

    @pl.loop(1, WALK)
    def _(d):
        y_copy(d, True).start()

    g_copy.wait_send()
    l_copy.wait_send()
    for k, (dz, dx) in enumerate(others):
        hr_copy(k, dz, dx).wait_send()

    @pl.loop(1, 16)
    def _(d):
        b_copy(d, True).wait_send()

    for ph, xg in ((0, xg1), (1, xg2)):
        for j in range(CHUNKS):
            for kind in range(9):
                ag_send(ph, xg, j, kind).wait_send()
            for kind in range(9, 19):
                sib(ph, xg, j, kind, core).wait_send()
            for kind in range(5):
                rs_copy(ph, j, kind).wait_send()

    @pl.loop(1, WALK)
    def _(d):
        s_copy(d, True).wait_send()
        z_copy(d, True).wait_send()

    @pl.loop(1, WALK)
    def _(d):
        y_copy(d, False).wait_recv()

    for p in range(WALK):
        both = yrecv[p].astype(f32)
        final[pl.ds(2 * p, 8, stride=64), :] = both[0:8]
        final[pl.ds(2 * p + 1, 8, stride=64), :] = both[8:16]
    out_ref[...] = final[...].reshape(8, 64, 128)[:, :, 0:100].astype(jnp.bfloat16)

    @pl.loop(1, WALK)
    def _(d):
        y_copy(d, True).wait_send()


def per_device(
    cholesky, half_rotated, green_half, walker, aux_noise, mf_shift, chol_index, walker_source
):
    bf16, f32 = jnp.bfloat16, jnp.float32
    vmem = pl.BlockSpec(memory_space=pltpu.VMEM)
    smem = pl.BlockSpec(memory_space=pltpu.SMEM)
    anyw = pl.BlockSpec(memory_space=pl.ANY)
    V = pltpu.VMEM
    D = pltpu.SemaphoreType.DMA
    moved = pl.pallas_call(
        body,
        out_shape=jax.ShapeDtypeStruct((8, 64, 100), bf16),
        in_specs=[anyw, anyw, vmem, vmem, smem, smem, smem, smem],
        out_specs=vmem,
        scratch_shapes=[
            V((4, 8, 64, 1024), bf16),
            V((TILES, 16, 64, 128), bf16),
            V((TILES, 16, 64, 128), bf16),
            V((2, CHUNKS, 2, 4, 2, 64, 128), bf16),
            V((2, CHUNKS, 2, 2, 64, 128), bf16),
            V((2, CHUNKS, 2, 2, 2, 64, 128), bf16),
            V((2, CHUNKS, 2, 64, 128), bf16),
            V((2, CHUNKS, 2, 64, 128), bf16),
            V((TILES, 64, 128), f32),
            V((512, 256), f32),
            V((8, 2, 128, 128), bf16),
            V((8, 2, 64, 128), bf16),
            V((4, 8, 128), f32),
            V((16, 8, 128), f32),
            V((512, 128), f32),
            V((WALK, 16, 128), bf16),
            V((WALK, 16, 128), bf16),
            V((WALK, 16, 128), bf16),
            V((WALK, 16, 128), bf16),
            V((8, 128), jnp.int32),
            V((WALK, 8, 128), jnp.int32),
            D((2, CHUNKS, 19)),
            D((2, CHUNKS, 19)),
            D((2, CHUNKS, 5)),
            D((2, CHUNKS, 5)),
            D((7,)),
            D((7,)),
            D((16,)),
            D((16,)),
            D((WALK,)),
            D((WALK,)),
            D((WALK,)),
            D((WALK,)),
            D((WALK,)),
            D((WALK,)),
            D((6,)),
        ],
        compiler_params=pltpu.CompilerParams(
            collective_id=0, has_side_effects=True, vmem_limit_bytes=40 * 1024 * 1024
        ),
        cost_estimate=pl.CostEstimate(
            flops=8_600_000_000, bytes_accessed=6_000_000, transcendentals=0
        ),
    )(
        cholesky.reshape(2, 8, 2, 64, 1024),
        jnp.pad(half_rotated, ((0, 0), (0, 12), (0, 0))),
        jnp.transpose(green_half, (0, 2, 1)),
        jnp.transpose(walker, (0, 2, 1)),
        jnp.transpose(aux_noise, (1, 0)),
        mf_shift,
        chol_index,
        walker_source,
    )
    return jnp.transpose(moved, (0, 2, 1))


def solution(mesh):
    placed = (
        P("chol", None, None),
        P("chol", None, None),
        P("walk", None, "chol"),
        P("walk", None, "chol"),
        P("walk", "chol"),
        P(),
        P("chol"),
        P("walk"),
    )
    return jax.shard_map(
        per_device, mesh=mesh, in_specs=placed, out_specs=P("walk", None, "chol"), check_vma=False
    )
```

```python
import jax
import jax.numpy as jnp
from jax import lax
from jax.experimental import pallas as pl
from jax.experimental.pallas import tpu as pltpu
from jax.sharding import PartitionSpec as P

MESH = pl.DeviceIdType.MESH
field_scale = 0.1
TILES = 7
SPANS = ((0, 2), (2, 2), (4, 2), (6, 1))
CHUNKS = len(SPANS)
WALK = 32
OCC = 100
OTHERS = ((1, 2), (0, 2), (1, 1), (1, 3), (0, 1), (0, 3), (1, 0))


def body(
    chol_ref, half_ref, green_ref, walker_ref, noise_ref, mean_ref, index_ref, source_ref,
    out_ref,
    lst, xg1, xg2, part, got, first, acc, hrg, gp, fb, btile, done, final,
    zsend, zrecv, ysend, yrecv, stile, sall, picks,
    green_in, walker_in, noise_in, mean_in, index_in, source_in,
    ag_s, ag_r, sib_s, sib_r, rs_s, rs_r, hr_s, hr_r, b_s, b_r, w_s, w_r, z_s, z_r, y_s, y_r,
    misc, in_sem,
):
    f32, bf16 = jnp.float32, jnp.bfloat16
    walk = lax.axis_index("walk")
    chol = lax.axis_index("chol")
    core = chol % 2
    chip = chol // 2
    x, z = chip % 4, chip // 4
    dev_sib = {"chol": chip * 2 + 1 - core}

    barrier = pltpu.get_barrier_semaphore()

    @pl.loop(1, WALK)
    def _(d):
        pl.semaphore_signal(
            barrier, inc=1, device_id={"walk": (walk + d) % WALK}, device_id_type=MESH
        )

    @pl.loop(1, 16)
    def _(d):
        pl.semaphore_signal(
            barrier, inc=1, device_id={"chol": (chol + d) % 16}, device_id_type=MESH
        )

    loads = [
        pltpu.make_async_copy(a, b, in_sem.at[n])
        for n, (a, b) in enumerate(
            (
                (source_ref, source_in), (walker_ref, walker_in), (green_ref, green_in),
                (index_ref, index_in), (noise_ref, noise_in), (mean_ref, mean_in),
            )
        )
    ]
    for load in loads:
        load.start()
    own_h = pltpu.make_async_copy(
        half_ref.at[:, :, pl.ds(pl.multiple_of(chip * 128, 128), 128)],
        hrg.at[chip, :, pl.ds(0, 112)],
        misc.at[1],
    )
    own_h.start()
    own_l = pltpu.make_async_copy(
        chol_ref.at[:, :, core], lst.at[pl.ds(2 * core, 2)], misc.at[0]
    )
    own_l.start()

    hrg[:, :, 112:128, :] = jnp.zeros((8, 2, 16, 128), bf16)

    row8 = lax.broadcasted_iota(jnp.int32, (8, 128), 0)
    lane8 = lax.broadcasted_iota(jnp.int32, (8, 128), 1)
    loads[0].wait()
    ids = jnp.zeros((8, 128), jnp.int32)
    for s in range(8):
        value = source_in[s]
        ids = jnp.where(row8 == s, (value // 8) * 16 + value % 8, ids)
    stile[...] = ids
    sall[walk] = ids

    loads[1].wait()
    done[...] = jnp.zeros_like(done)
    done[:, :, 0:OCC] = walker_in[...].astype(f32)
    lanes = lax.broadcasted_iota(jnp.int32, (64, 128), 1)
    shifted = [
        pltpu.roll(done[w], (OCC * w) % 128, 1) if w else done[w] for w in range(8)
    ]
    for t in range(TILES):
        tile = jnp.zeros((64, 128), f32)
        for w in range(8):
            low, high = OCC * w - 128 * t, OCC * (w + 1) - 128 * t
            if high > 0 and low < 128:
                tile = jnp.where((lanes >= low) & (lanes < high), shifted[w], tile)
        xg1[t, chol] = tile.astype(bf16)
    loads[2].wait()
    gp[:, core] = jnp.zeros((8, 64, 128), bf16)
    gp[:, core, :, 0:OCC] = green_in[...]

    pl.semaphore_wait(barrier, 15 + WALK - 1)

    def remote(src, dst, ssem, rsem, dev):
        return pltpu.make_async_remote_copy(
            src_ref=src, dst_ref=dst, send_sem=ssem, recv_sem=rsem,
            device_id=dev, device_id_type=MESH,
        )

    def chip_to(dz, dx):
        return ((z + dz) % 2) * 4 + (x + dx) % 4

    def chip_from(dz, dx):
        return ((z + dz) % 2) * 4 + (x + 4 - dx) % 4

    g_copy = remote(gp.at[:, core], gp.at[:, core], misc.at[2], misc.at[3], dev_sib)
    g_copy.start()
    g_got = remote(gp.at[:, 1 - core], gp.at[:, 1 - core], misc.at[2], misc.at[3], dev_sib)

    def hr_copy(k):
        there = chip_to(*OTHERS[k])
        return remote(
            half_ref.at[:, :, pl.ds(pl.multiple_of(there * 128, 128), 128)],
            hrg.at[chip, :, pl.ds(0, 112)],
            hr_s.at[k], hr_r.at[k], {"chol": there * 2 + core},
        )

    def hr_got(k):
        ref = hrg.at[chip_from(*OTHERS[k]), :, pl.ds(0, 112)]
        return remote(ref, ref, hr_s.at[k], hr_r.at[k], dev_sib)

    for k in range(7):
        hr_copy(k).start()

    l_copy = remote(
        chol_ref.at[:, :, 1 - core], lst.at[pl.ds(2 * core, 2)], misc.at[4], misc.at[5], dev_sib
    )
    l_got = remote(
        lst.at[pl.ds(2 * (1 - core), 2)], lst.at[pl.ds(2 * (1 - core), 2)],
        misc.at[4], misc.at[5], dev_sib,
    )

    def s_copy(d, sending):
        there = (walk + d) % WALK if sending else (walk + WALK - d) % WALK
        return remote(
            stile, sall.at[walk] if sending else sall.at[there],
            w_s.at[d], w_r.at[d], {"walk": there},
        )

    def tiles(j):
        return pl.ds(SPANS[j][0], SPANS[j][1])

    def ag_send(ph, xg, j, k):
        ref = xg.at[tiles(j), chol]
        return remote(
            ref, ref, ag_s.at[ph, j, k], ag_r.at[ph, j, k],
            {"chol": chip_to(*OTHERS[k]) * 2 + core},
        )

    def ag_got(ph, xg, j, k):
        ref = xg.at[tiles(j), chip_from(*OTHERS[k]) * 2 + core]
        return remote(ref, ref, ag_s.at[ph, j, k], ag_r.at[ph, j, k], dev_sib)

    def sib(ph, xg, j, k, cc):
        there = chip if k == 7 else chip_from(*OTHERS[k])
        ref = xg.at[tiles(j), there * 2 + cc]
        return remote(ref, ref, sib_s.at[ph, j, k], sib_r.at[ph, j, k], dev_sib)

    def ag_start(ph, xg, j):
        for k in range(7):
            ag_send(ph, xg, j, k).start()
        sib(ph, xg, j, 7, core).start()

    def ag_relay(ph, xg, j):
        for k in reversed(range(7)):
            ag_got(ph, xg, j, k).wait_recv()
            sib(ph, xg, j, k, core).start()

    def ag_fin(ph, xg, j):
        for k in range(8):
            sib(ph, xg, j, k, 1 - core).wait_recv()

    def rs_copy(ph, j, k):
        there = chip_to(*OTHERS[k])
        return remote(
            part.at[ph, there, tiles(j)], got.at[ph, k, tiles(j)],
            rs_s.at[ph, j, k], rs_r.at[ph, j, k], {"chol": there * 2 + core},
        )

    def rs_start(ph, j):
        for k in range(7):
            rs_copy(ph, j, k).start()

    def rs_fin(ph, j):
        for k in range(7):
            rs_copy(ph, j, k).wait_recv()
        total = part[ph, chip, tiles(j)].astype(f32)
        for k in range(7):
            total = total + got[ph, k, tiles(j)].astype(f32)
        return total

    def matmul(ph, xg, j):
        start, size = SPANS[j]
        both = jnp.concatenate(
            [xg[start + n].reshape(1024, 128) for n in range(size)], axis=1
        )
        columns = pl.ds(0, 128 * size)
        for g in range(4):
            product = jnp.dot(
                lst[g].reshape(512, 1024), both, preferred_element_type=f32
            )
            scale = jnp.concatenate(
                [fb[g, pl.ds(start + n, 1), :] for n in range(size)], axis=1
            )
            if g == 0:
                acc[:, columns] = product * scale
            else:
                acc[:, columns] += product * scale
        for q in range(8):
            for n in range(size):
                part[ph, q, start + n] = acc[
                    pl.ds(64 * q, 64), pl.ds(128 * n, 128)
                ].astype(bf16)

    for j in range(CHUNKS):
        ag_start(0, xg1, j)
    l_copy.start()

    @pl.loop(1, WALK)
    def _(d):
        s_copy(d, True).start()

    for load in loads[3:]:
        load.wait()
    own_h.wait()
    g_got.wait_recv()
    for k in range(7):
        hr_got(k).wait_recv()

    eye = (
        lax.broadcasted_iota(jnp.int32, (128, 128), 0)
        == lax.broadcasted_iota(jnp.int32, (128, 128), 1)
    ).astype(f32)
    greens = gp[...].reshape(1024, 128)

    def one_vector(v, tile):
        source, which = v // 2, v % 2
        product = jnp.dot(greens, hrg[source, which], preferred_element_type=f32)
        picked = jnp.sum(product.reshape(8, 128, 128) * eye[None], axis=1)
        value = jnp.sum(picked, axis=1, keepdims=True)
        return jnp.where(lane8 == source * 4 + core * 2 + which, field_scale * value, tile)

    tile = lax.fori_loop(0, 16, one_vector, jnp.zeros((8, 128), f32))
    for which in range(2):
        shift = mean_in[index_in[which]]
        for w in range(8):
            tile = tile + jnp.where(
                (row8 == w) & (lane8 == chol * 2 + which),
                noise_in[which, w] - field_scale * shift, 0.0,
            )
    btile[chol] = tile

    def b_copy(d, sending):
        there = (chol + d) % 16 if sending else (chol + 16 - d) % 16
        slot = chol if sending else there
        return remote(
            btile.at[slot], btile.at[slot], b_s.at[d], b_r.at[d], {"chol": there}
        )

    @pl.loop(1, 16)
    def _(d):
        b_copy(d, True).start()

    ag_relay(0, xg1, 0)

    @pl.loop(1, WALK)
    def _(d):
        s_copy(d, False).wait_recv()

    low = sall[...]
    wanted = jnp.stack([low, low + 8], axis=1).reshape(WALK * 16, 128)
    wide = lax.broadcasted_iota(jnp.int32, (WALK * 16, 128), 1)
    for b in range(4):
        picks[b] = jnp.where(wanted == wide + 128 * b, 1.0, 0.0).astype(bf16)

    ag_relay(0, xg1, 1)

    @pl.loop(1, 16)
    def _(d):
        b_copy(d, False).wait_recv()

    field = btile[0]
    for c in range(1, 16):
        field = field + btile[c]
    for g in range(4):
        value = jnp.sum(
            jnp.where(lane8 == chip * 4 + g, field, 0.0), axis=1, keepdims=True
        )
        for t in range(TILES):
            column = lane8 + 128 * t
            mine = (column >= OCC * row8) & (column < OCC * (row8 + 1))
            fb[g, pl.ds(t, 1), :] = jnp.sum(
                jnp.where(mine, value, 0.0), axis=0, keepdims=True
            )

    own_l.wait()
    l_got.wait_recv()

    def mm1(j):
        ag_fin(0, xg1, j)
        matmul(0, xg1, j)
        rs_start(0, j)

    def turn(j):
        term = field_scale * rs_fin(0, j)
        first[tiles(j)] = term
        xg2[tiles(j), chol] = term.astype(bf16)
        ag_start(1, xg2, j)

    def mm2(j):
        ag_fin(1, xg2, j)
        matmul(1, xg2, j)
        rs_start(1, j)

    def finish(j):
        done_tiles = (
            xg1[tiles(j), chol].astype(f32)
            + first[tiles(j)]
            + (0.5 * field_scale) * rs_fin(1, j)
        )
        first[tiles(j)] = done_tiles

    mm1(0)
    ag_relay(0, xg1, 2)
    mm1(1)
    ag_relay(0, xg1, 3)
    turn(0)
    mm1(2)
    turn(1)
    mm1(3)
    ag_relay(1, xg2, 0)
    turn(2)
    ag_relay(1, xg2, 1)
    mm2(0)
    turn(3)
    ag_relay(1, xg2, 2)
    mm2(1)
    ag_relay(1, xg2, 3)
    finish(0)
    mm2(2)
    finish(1)
    mm2(3)
    finish(2)
    finish(3)

    for w in range(8):
        t, start = (OCC * w) // 128, (OCC * w) % 128
        if start:
            mixed = jnp.where(lanes >= start, first[t], first[min(t + 1, TILES - 1)])
            mixed = pltpu.roll(mixed, 128 - start, 1)
        else:
            mixed = first[t]
        final[pl.ds(64 * w, 64)] = mixed

    for p in range(WALK):
        zsend[p] = jnp.concatenate(
            [final[pl.ds(2 * p, 8, stride=64), :], final[pl.ds(2 * p + 1, 8, stride=64), :]],
            axis=0,
        ).astype(bf16)
    zrecv[walk] = zsend[walk]

    def z_copy(d, sending):
        there = (walk + d) % WALK if sending else (walk + WALK - d) % WALK
        return remote(
            zsend.at[there], zrecv.at[walk] if sending else zrecv.at[there],
            z_s.at[d], z_r.at[d], {"walk": there},
        )

    def y_copy(d, sending):
        there = (walk + d) % WALK if sending else (walk + WALK - d) % WALK
        return remote(
            ysend.at[there], yrecv.at[walk] if sending else yrecv.at[there],
            y_s.at[d], y_r.at[d], {"walk": there},
        )

    @pl.loop(1, WALK)
    def _(d):
        z_copy(d, True).start()

    @pl.loop(1, WALK)
    def _(d):
        z_copy(d, False).wait_recv()

    here = zrecv[...].reshape(WALK * 16, 128)
    taken = jnp.dot(picks[0], here[0:128], preferred_element_type=f32)
    for b in range(1, 4):
        taken = taken + jnp.dot(
            picks[b], here[128 * b : 128 * (b + 1)], preferred_element_type=f32
        )
    ysend[...] = taken.astype(bf16).reshape(WALK, 16, 128)
    yrecv[walk] = ysend[walk]

    @pl.loop(1, WALK)
    def _(d):
        y_copy(d, True).start()

    g_copy.wait_send()
    l_copy.wait_send()
    for k in range(7):
        hr_copy(k).wait_send()

    @pl.loop(1, 16)
    def _(d):
        b_copy(d, True).wait_send()

    for ph, xg in ((0, xg1), (1, xg2)):
        for j in range(CHUNKS):
            for k in range(7):
                ag_send(ph, xg, j, k).wait_send()
                rs_copy(ph, j, k).wait_send()
            for k in range(8):
                sib(ph, xg, j, k, core).wait_send()

    @pl.loop(1, WALK)
    def _(d):
        s_copy(d, True).wait_send()
        z_copy(d, True).wait_send()

    @pl.loop(1, WALK)
    def _(d):
        y_copy(d, False).wait_recv()

    for p in range(WALK):
        both = yrecv[p].astype(f32)
        final[pl.ds(2 * p, 8, stride=64), :] = both[0:8]
        final[pl.ds(2 * p + 1, 8, stride=64), :] = both[8:16]
    out_ref[...] = final[...].reshape(8, 64, 128)[:, :, 0:OCC].astype(bf16)

    @pl.loop(1, WALK)
    def _(d):
        y_copy(d, True).wait_send()


def per_device(
    cholesky, half_rotated, green_half, walker, aux_noise, mf_shift, chol_index, walker_source
):
    bf16, f32, i32 = jnp.bfloat16, jnp.float32, jnp.int32
    V, S, D = pltpu.VMEM, pltpu.SMEM, pltpu.SemaphoreType.DMA
    moved = pl.pallas_call(
        body,
        out_shape=jax.ShapeDtypeStruct((8, 64, OCC), bf16),
        in_specs=[pl.BlockSpec(memory_space=pltpu.HBM)] * 8,
        out_specs=pl.BlockSpec(memory_space=pltpu.VMEM),
        scratch_shapes=[
            V((4, 8, 64, 1024), bf16),
            V((TILES, 16, 64, 128), bf16),
            V((TILES, 16, 64, 128), bf16),
            V((2, 8, TILES, 64, 128), bf16),
            V((2, 7, TILES, 64, 128), bf16),
            V((TILES, 64, 128), f32),
            V((512, 256), f32),
            V((8, 2, 128, 128), bf16),
            V((8, 2, 64, 128), bf16),
            V((4, 8, 128), f32),
            V((16, 8, 128), f32),
            V((8, 64, 128), f32),
            V((512, 128), f32),
            V((WALK, 16, 128), bf16),
            V((WALK, 16, 128), bf16),
            V((WALK, 16, 128), bf16),
            V((WALK, 16, 128), bf16),
            V((8, 128), i32),
            V((WALK, 8, 128), i32),
            V((4, WALK * 16, 128), bf16),
            V((8, 64, OCC), bf16),
            V((8, 64, OCC), bf16),
            S((2, 8), f32),
            S((4000,), f32),
            S((2,), i32),
            S((8,), i32),
            D((2, CHUNKS, 7)),
            D((2, CHUNKS, 7)),
            D((2, CHUNKS, 8)),
            D((2, CHUNKS, 8)),
            D((2, CHUNKS, 7)),
            D((2, CHUNKS, 7)),
            D((7,)),
            D((7,)),
            D((16,)),
            D((16,)),
            D((WALK,)),
            D((WALK,)),
            D((WALK,)),
            D((WALK,)),
            D((WALK,)),
            D((WALK,)),
            D((6,)),
            D((6,)),
        ],
        compiler_params=pltpu.CompilerParams(
            collective_id=0, has_side_effects=True, vmem_limit_bytes=48 * 1024 * 1024
        ),
        cost_estimate=pl.CostEstimate(
            flops=8_600_000_000, bytes_accessed=6_000_000, transcendentals=0
        ),
    )(
        cholesky.reshape(2, 8, 2, 64, 1024),
        jnp.pad(half_rotated, ((0, 0), (0, 12), (0, 0))),
        jnp.transpose(green_half, (0, 2, 1)),
        jnp.transpose(walker, (0, 2, 1)),
        jnp.transpose(aux_noise, (1, 0)),
        mf_shift,
        chol_index,
        walker_source,
    )
    return jnp.transpose(moved, (0, 2, 1))


def solution(mesh):
    placed = (
        P("chol", None, None),
        P("chol", None, None),
        P("walk", None, "chol"),
        P("walk", None, "chol"),
        P("walk", "chol"),
        P(),
        P("chol"),
        P("walk"),
    )
    return jax.shard_map(
        per_device, mesh=mesh, in_specs=placed, out_specs=P("walk", None, "chol"), check_vma=False
    )
```

```python
import jax
import jax.numpy as jnp
from jax import lax
from jax.experimental import pallas as pl
from jax.experimental.pallas import tpu as pltpu
from jax.sharding import PartitionSpec as P

MESH = pl.DeviceIdType.MESH
field_scale = 0.1
TILES = 7
SPANS = ((0, 2), (2, 2), (4, 2), (6, 1))
CHUNKS = len(SPANS)
WALK = 32
OCC = 100
OTHERS = ((1, 2), (0, 2), (1, 1), (1, 3), (0, 1), (0, 3), (1, 0))


def body(
    chol_ref, half_ref, green_ref, walker_ref, noise_ref, mean_ref, index_ref, source_ref,
    out_ref,
    lst, xg1, xg2, part, got, first, acc, hrg, gp, fb, btile, final,
    zsend, zrecv, ysend, yrecv, stile, sall, fall, fsel,
    green_in, walker_in, noise_in, mean_in, index_in, source_in,
    ag_s, ag_r, sib_s, sib_r, rs_s, rs_r, hr_s, hr_r, b_s, b_r, w_s, w_r, z_s, z_r, y_s, y_r, f_s, f_r,
    misc, in_sem,
):
    f32, bf16 = jnp.float32, jnp.bfloat16
    walk = lax.axis_index("walk")
    chol = lax.axis_index("chol")
    core = chol % 2
    chip = chol // 2
    x, z = chip % 4, chip // 4
    dev_sib = {"chol": chip * 2 + 1 - core}

    barrier = pltpu.get_barrier_semaphore()

    @pl.loop(1, WALK)
    def _(d):
        pl.semaphore_signal(
            barrier, inc=1, device_id={"walk": (walk + d) % WALK}, device_id_type=MESH
        )

    @pl.loop(1, 16)
    def _(d):
        pl.semaphore_signal(
            barrier, inc=1, device_id={"chol": (chol + d) % 16}, device_id_type=MESH
        )

    loads = [
        pltpu.make_async_copy(a, b, in_sem.at[n])
        for n, (a, b) in enumerate(
            (
                (source_ref, source_in), (walker_ref, walker_in), (green_ref, green_in),
                (index_ref, index_in), (noise_ref, noise_in), (mean_ref, mean_in),
            )
        )
    ]
    for load in loads:
        load.start()
    own_h = pltpu.make_async_copy(
        half_ref.at[:, :, pl.ds(pl.multiple_of(chip * 128, 128), 128)],
        hrg.at[chip, :, pl.ds(0, 112)],
        misc.at[1],
    )
    own_h.start()
    own_l = pltpu.make_async_copy(
        chol_ref.at[:, :, core], lst.at[pl.ds(2 * core, 2)], misc.at[0]
    )
    own_l.start()

    hrg[:, :, 112:128, :] = jnp.zeros((8, 2, 16, 128), bf16)

    row8 = lax.broadcasted_iota(jnp.int32, (8, 128), 0)
    lane8 = lax.broadcasted_iota(jnp.int32, (8, 128), 1)
    loads[0].wait()
    ids = jnp.zeros((8, 128), jnp.int32)
    for s in range(8):
        value = source_in[s]
        ids = jnp.where(row8 == s, (value // 8) * 16 + value % 8, ids)
    stile[...] = ids
    sall[walk] = ids

    loads[1].wait()
    final[...] = jnp.zeros_like(final)
    final[:, 0:OCC] = walker_in[...].astype(f32).reshape(512, OCC)
    for p in range(WALK):
        zsend[p] = jnp.concatenate(
            [final[pl.ds(2 * p, 8, stride=64), :], final[pl.ds(2 * p + 1, 8, stride=64), :]],
            axis=0,
        ).astype(bf16)
    zrecv[walk] = zsend[walk]
    loads[2].wait()
    gp[:, core] = jnp.zeros((8, 64, 128), bf16)
    gp[:, core, :, 0:OCC] = green_in[...]

    pl.semaphore_wait(barrier, 15 + WALK - 1)

    def remote(src, dst, ssem, rsem, dev):
        return pltpu.make_async_remote_copy(
            src_ref=src, dst_ref=dst, send_sem=ssem, recv_sem=rsem,
            device_id=dev, device_id_type=MESH,
        )

    def chip_to(dz, dx):
        return ((z + dz) % 2) * 4 + (x + dx) % 4

    def chip_from(dz, dx):
        return ((z + dz) % 2) * 4 + (x + 4 - dx) % 4

    def walk_peer(d, sending):
        return (walk + d) % WALK if sending else (walk + WALK - d) % WALK

    def walk_copy(src, dst, ssem, rsem, d, sending):
        there = walk_peer(d, sending)
        return remote(src, dst, ssem.at[d], rsem.at[d], {"walk": there})

    def s_copy(d, sending):
        slot = walk if sending else walk_peer(d, sending)
        return walk_copy(stile, sall.at[slot], w_s, w_r, d, sending)

    def z_copy(d, sending):
        there = walk_peer(d, sending)
        slot = walk if sending else there
        return walk_copy(zsend.at[there], zrecv.at[slot], z_s, z_r, d, sending)

    def y_copy(d, sending):
        there = walk_peer(d, sending)
        slot = walk if sending else there
        return walk_copy(ysend.at[there], yrecv.at[slot], y_s, y_r, d, sending)

    def f_copy(d, sending):
        slot = walk if sending else walk_peer(d, sending)
        ref = fall.at[pl.ds(pl.multiple_of(8 * slot, 8), 8)]
        return walk_copy(ref, ref, f_s, f_r, d, sending)

    @pl.loop(1, WALK)
    def _(d):
        z_copy(d, True).start()
        s_copy(d, True).start()

    g_copy = remote(gp.at[:, core], gp.at[:, core], misc.at[2], misc.at[3], dev_sib)
    g_copy.start()
    g_got = remote(gp.at[:, 1 - core], gp.at[:, 1 - core], misc.at[2], misc.at[3], dev_sib)

    def hr_copy(k):
        there = chip_to(*OTHERS[k])
        return remote(
            half_ref.at[:, :, pl.ds(pl.multiple_of(there * 128, 128), 128)],
            hrg.at[chip, :, pl.ds(0, 112)],
            hr_s.at[k], hr_r.at[k], {"chol": there * 2 + core},
        )

    def hr_got(k):
        ref = hrg.at[chip_from(*OTHERS[k]), :, pl.ds(0, 112)]
        return remote(ref, ref, hr_s.at[k], hr_r.at[k], dev_sib)

    for k in range(7):
        hr_copy(k).start()

    l_copy = remote(
        chol_ref.at[:, :, 1 - core], lst.at[pl.ds(2 * core, 2)], misc.at[4], misc.at[5], dev_sib
    )
    l_got = remote(
        lst.at[pl.ds(2 * (1 - core), 2)], lst.at[pl.ds(2 * (1 - core), 2)],
        misc.at[4], misc.at[5], dev_sib,
    )

    def tiles(j):
        return pl.ds(SPANS[j][0], SPANS[j][1])

    def ag_send(ph, xg, j, k):
        ref = xg.at[tiles(j), chol]
        return remote(
            ref, ref, ag_s.at[ph, j, k], ag_r.at[ph, j, k],
            {"chol": chip_to(*OTHERS[k]) * 2 + core},
        )

    def ag_got(ph, xg, j, k):
        ref = xg.at[tiles(j), chip_from(*OTHERS[k]) * 2 + core]
        return remote(ref, ref, ag_s.at[ph, j, k], ag_r.at[ph, j, k], dev_sib)

    def sib(ph, xg, j, k, cc):
        there = chip if k == 7 else chip_from(*OTHERS[k])
        ref = xg.at[tiles(j), there * 2 + cc]
        return remote(ref, ref, sib_s.at[ph, j, k], sib_r.at[ph, j, k], dev_sib)

    def ag_start(ph, xg, j):
        for k in range(7):
            ag_send(ph, xg, j, k).start()
        sib(ph, xg, j, 7, core).start()

    def ag_relay(ph, xg, j):
        for k in reversed(range(7)):
            ag_got(ph, xg, j, k).wait_recv()
            sib(ph, xg, j, k, core).start()

    def ag_fin(ph, xg, j):
        for k in range(8):
            sib(ph, xg, j, k, 1 - core).wait_recv()

    def rs_copy(ph, j, k):
        there = chip_to(*OTHERS[k])
        return remote(
            part.at[ph, there, tiles(j)], got.at[ph, k, tiles(j)],
            rs_s.at[ph, j, k], rs_r.at[ph, j, k], {"chol": there * 2 + core},
        )

    def rs_start(ph, j):
        for k in range(7):
            rs_copy(ph, j, k).start()

    def rs_fin(ph, j):
        for k in range(7):
            rs_copy(ph, j, k).wait_recv()
        total = part[ph, chip, tiles(j)].astype(f32)
        for k in range(7):
            total = total + got[ph, k, tiles(j)].astype(f32)
        return total

    def matmul(ph, xg, j):
        start, size = SPANS[j]
        both = jnp.concatenate(
            [xg[start + n].reshape(1024, 128) for n in range(size)], axis=1
        )
        columns = pl.ds(0, 128 * size)
        for g in range(4):
            product = jnp.dot(
                lst[g].reshape(512, 1024), both, preferred_element_type=f32
            )
            scale = jnp.concatenate(
                [fb[g, pl.ds(start + n, 1), :] for n in range(size)], axis=1
            )
            if g == 0:
                acc[:, columns] = product * scale
            else:
                acc[:, columns] += product * scale
        for q in range(8):
            for n in range(size):
                part[ph, q, start + n] = acc[
                    pl.ds(64 * q, 64), pl.ds(128 * n, 128)
                ].astype(bf16)

    l_copy.start()

    @pl.loop(1, WALK)
    def _(d):
        s_copy(d, False).wait_recv()

    low = sall[...]
    wanted = jnp.stack([low, low + 8], axis=1).reshape(WALK * 16, 128)
    wide = lax.broadcasted_iota(jnp.int32, (WALK * 16, 128), 1)
    picks = [jnp.where(wanted == wide + 128 * b, 1.0, 0.0).astype(bf16) for b in range(4)]

    @pl.loop(1, WALK)
    def _(d):
        z_copy(d, False).wait_recv()

    here = zrecv[...].reshape(WALK * 16, 128)
    taken = jnp.dot(picks[0], here[0:128], preferred_element_type=f32)
    for b in range(1, 4):
        taken = taken + jnp.dot(
            picks[b], here[128 * b : 128 * (b + 1)], preferred_element_type=f32
        )
    ysend[...] = taken.astype(bf16).reshape(WALK, 16, 128)
    yrecv[walk] = ysend[walk]

    @pl.loop(1, WALK)
    def _(d):
        y_copy(d, True).start()

    for load in loads[3:]:
        load.wait()
    own_h.wait()
    g_got.wait_recv()
    for k in range(7):
        hr_got(k).wait_recv()

    eye = (
        lax.broadcasted_iota(jnp.int32, (128, 128), 0)
        == lax.broadcasted_iota(jnp.int32, (128, 128), 1)
    ).astype(f32)
    greens = gp[...].reshape(1024, 128)

    def one_vector(v, tile):
        source, which = v // 2, v % 2
        product = jnp.dot(greens, hrg[source, which], preferred_element_type=f32)
        picked = jnp.sum(product.reshape(8, 128, 128) * eye[None], axis=1)
        value = jnp.sum(picked, axis=1, keepdims=True)
        return jnp.where(lane8 == source * 4 + core * 2 + which, field_scale * value, tile)

    tile = lax.fori_loop(0, 16, one_vector, jnp.zeros((8, 128), f32))
    for which in range(2):
        shift = mean_in[index_in[which]]
        for w in range(8):
            tile = tile + jnp.where(
                (row8 == w) & (lane8 == chol * 2 + which),
                noise_in[which, w] - field_scale * shift, 0.0,
            )
    btile[chol] = tile

    def b_copy(d, sending):
        there = (chol + d) % 16 if sending else (chol + 16 - d) % 16
        slot = chol if sending else there
        return remote(
            btile.at[slot], btile.at[slot], b_s.at[d], b_r.at[d], {"chol": there}
        )

    @pl.loop(1, 16)
    def _(d):
        b_copy(d, True).start()

    @pl.loop(1, 16)
    def _(d):
        b_copy(d, False).wait_recv()

    field = btile[0]
    for c in range(1, 16):
        field = field + btile[c]
    fall[pl.ds(pl.multiple_of(8 * walk, 8), 8)] = field

    @pl.loop(1, WALK)
    def _(d):
        f_copy(d, True).start()

    @pl.loop(1, WALK)
    def _(d):
        y_copy(d, False).wait_recv()

    for p in range(WALK):
        both = yrecv[p].astype(f32)
        final[pl.ds(2 * p, 8, stride=64), :] = both[0:8]
        final[pl.ds(2 * p + 1, 8, stride=64), :] = both[8:16]
    lanes = lax.broadcasted_iota(jnp.int32, (64, 128), 1)
    shifted = [final[pl.ds(64 * w, 64)] for w in range(8)]
    shifted = [
        pltpu.roll(v, (OCC * w) % 128, 1) if w else v for w, v in enumerate(shifted)
    ]
    for t in range(TILES):
        tile = jnp.zeros((64, 128), f32)
        for w in range(8):
            left, right = OCC * w - 128 * t, OCC * (w + 1) - 128 * t
            if right > 0 and left < 128:
                tile = jnp.where((lanes >= left) & (lanes < right), shifted[w], tile)
        xg1[t, chol] = tile.astype(bf16)
    for j in range(CHUNKS):
        ag_start(0, xg1, j)

    ag_relay(0, xg1, 0)

    @pl.loop(1, WALK)
    def _(d):
        f_copy(d, False).wait_recv()

    for s in range(8):
        fsel[pl.ds(s, 1), :] = fall[pl.ds(source_in[s], 1), :]
    field = fsel[...]
    for g in range(4):
        value = jnp.sum(
            jnp.where(lane8 == chip * 4 + g, field, 0.0), axis=1, keepdims=True
        )
        for t in range(TILES):
            column = lane8 + 128 * t
            mine = (column >= OCC * row8) & (column < OCC * (row8 + 1))
            fb[g, pl.ds(t, 1), :] = jnp.sum(
                jnp.where(mine, value, 0.0), axis=0, keepdims=True
            )

    ag_relay(0, xg1, 1)
    own_l.wait()
    l_got.wait_recv()

    def mm1(j):
        ag_fin(0, xg1, j)
        matmul(0, xg1, j)
        rs_start(0, j)

    def turn(j):
        term = field_scale * rs_fin(0, j)
        first[tiles(j)] = term
        xg2[tiles(j), chol] = term.astype(bf16)
        ag_start(1, xg2, j)

    def mm2(j):
        ag_fin(1, xg2, j)
        matmul(1, xg2, j)
        rs_start(1, j)

    def finish(j):
        done_tiles = (
            xg1[tiles(j), chol].astype(f32)
            + first[tiles(j)]
            + (0.5 * field_scale) * rs_fin(1, j)
        )
        first[tiles(j)] = done_tiles

    mm1(0)
    ag_relay(0, xg1, 2)
    mm1(1)
    ag_relay(0, xg1, 3)
    turn(0)
    mm1(2)
    turn(1)
    mm1(3)
    ag_relay(1, xg2, 0)
    turn(2)
    ag_relay(1, xg2, 1)
    mm2(0)
    turn(3)
    ag_relay(1, xg2, 2)
    mm2(1)
    ag_relay(1, xg2, 3)
    finish(0)
    mm2(2)
    finish(1)
    mm2(3)
    finish(2)
    finish(3)

    for w in range(8):
        t, start = (OCC * w) // 128, (OCC * w) % 128
        if start:
            mixed = jnp.where(lanes >= start, first[t], first[min(t + 1, TILES - 1)])
            mixed = pltpu.roll(mixed, 128 - start, 1)
        else:
            mixed = first[t]
        out_ref[w] = mixed[:, 0:OCC].astype(bf16)

    g_copy.wait_send()
    l_copy.wait_send()
    for k in range(7):
        hr_copy(k).wait_send()

    @pl.loop(1, 16)
    def _(d):
        b_copy(d, True).wait_send()

    for ph, xg in ((0, xg1), (1, xg2)):
        for j in range(CHUNKS):
            for k in range(7):
                ag_send(ph, xg, j, k).wait_send()
                rs_copy(ph, j, k).wait_send()
            for k in range(8):
                sib(ph, xg, j, k, core).wait_send()

    @pl.loop(1, WALK)
    def _(d):
        s_copy(d, True).wait_send()
        z_copy(d, True).wait_send()
        y_copy(d, True).wait_send()
        f_copy(d, True).wait_send()


def per_device(
    cholesky, half_rotated, green_half, walker, aux_noise, mf_shift, chol_index, walker_source
):
    bf16, f32, i32 = jnp.bfloat16, jnp.float32, jnp.int32
    V, S, D = pltpu.VMEM, pltpu.SMEM, pltpu.SemaphoreType.DMA
    moved = pl.pallas_call(
        body,
        out_shape=jax.ShapeDtypeStruct((8, 64, OCC), bf16),
        in_specs=[pl.BlockSpec(memory_space=pltpu.HBM)] * 8,
        out_specs=pl.BlockSpec(memory_space=pltpu.VMEM),
        scratch_shapes=[
            V((4, 8, 64, 1024), bf16),
            V((TILES, 16, 64, 128), bf16),
            V((TILES, 16, 64, 128), bf16),
            V((2, 8, TILES, 64, 128), bf16),
            V((2, 7, TILES, 64, 128), bf16),
            V((TILES, 64, 128), f32),
            V((512, 256), f32),
            V((8, 2, 128, 128), bf16),
            V((8, 2, 64, 128), bf16),
            V((4, 8, 128), f32),
            V((16, 8, 128), f32),
            V((512, 128), f32),
            V((WALK, 16, 128), bf16),
            V((WALK, 16, 128), bf16),
            V((WALK, 16, 128), bf16),
            V((WALK, 16, 128), bf16),
            V((8, 128), i32),
            V((WALK, 8, 128), i32),
            V((256, 128), f32),
            V((8, 128), f32),
            V((8, 64, OCC), bf16),
            V((8, 64, OCC), bf16),
            S((2, 8), f32),
            S((4000,), f32),
            S((2,), i32),
            S((8,), i32),
            D((2, CHUNKS, 7)),
            D((2, CHUNKS, 7)),
            D((2, CHUNKS, 8)),
            D((2, CHUNKS, 8)),
            D((2, CHUNKS, 7)),
            D((2, CHUNKS, 7)),
            D((7,)),
            D((7,)),
            D((16,)),
            D((16,)),
            D((WALK,)),
            D((WALK,)),
            D((WALK,)),
            D((WALK,)),
            D((WALK,)),
            D((WALK,)),
            D((WALK,)),
            D((WALK,)),
            D((6,)),
            D((6,)),
        ],
        compiler_params=pltpu.CompilerParams(
            collective_id=0, has_side_effects=True, vmem_limit_bytes=64 * 1024 * 1024
        ),
        cost_estimate=pl.CostEstimate(
            flops=8_600_000_000, bytes_accessed=6_000_000, transcendentals=0
        ),
    )(
        cholesky.reshape(2, 8, 2, 64, 1024),
        jnp.pad(half_rotated, ((0, 0), (0, 12), (0, 0))),
        jnp.transpose(green_half, (0, 2, 1)),
        jnp.transpose(walker, (0, 2, 1)),
        jnp.transpose(aux_noise, (1, 0)),
        mf_shift,
        chol_index,
        walker_source,
    )
    return jnp.transpose(moved, (0, 2, 1))


def solution(mesh):
    placed = (
        P("chol", None, None),
        P("chol", None, None),
        P("walk", None, "chol"),
        P("walk", None, "chol"),
        P("walk", "chol"),
        P(),
        P("chol"),
        P("walk"),
    )
    return jax.shard_map(
        per_device, mesh=mesh, in_specs=placed, out_specs=P("walk", None, "chol"), check_vma=False
    )
```

```python
import jax
import jax.numpy as jnp
from jax import lax
from jax.experimental import pallas as pl
from jax.experimental.pallas import tpu as pltpu
from jax.sharding import PartitionSpec as P

MESH = pl.DeviceIdType.MESH
field_scale = 0.1
TILES = 7
SPANS = ((0, 2), (2, 2), (4, 2), (6, 1))
CHUNKS = len(SPANS)
WALK = 32
OCC = 100
OTHERS = ((1, 2), (0, 2), (1, 1), (1, 3), (0, 1), (0, 3), (1, 0))


def body(
    chol_ref, half_ref, green_ref, walker_ref, noise_ref, mean_ref, index_ref, source_ref,
    out_ref,
    lst, xg1, xg2, part, got, first, acc, hrg, gp, fb, btile, final,
    zsend, zrecv, ysend, yrecv, stile, sall, fall, fsel,
    green_in, walker_in, noise_in, mean_in, index_in, source_in,
    ag_s, ag_r, sib_s, sib_r, rs_s, rs_r, hr_s, hr_r, b_s, b_r, w_s, w_r, z_s, z_r, y_s, y_r, f_s, f_r,
    misc, in_sem,
):
    f32, bf16 = jnp.float32, jnp.bfloat16
    walk = lax.axis_index("walk")
    chol = lax.axis_index("chol")
    core = chol % 2
    chip = chol // 2
    x, z = chip % 4, chip // 4
    dev_sib = {"chol": chip * 2 + 1 - core}

    barrier = pltpu.get_barrier_semaphore()

    @pl.loop(1, WALK)
    def _(d):
        pl.semaphore_signal(
            barrier, inc=1, device_id={"walk": (walk + d) % WALK}, device_id_type=MESH
        )

    @pl.loop(1, 16)
    def _(d):
        pl.semaphore_signal(
            barrier, inc=1, device_id={"chol": (chol + d) % 16}, device_id_type=MESH
        )

    loads = [
        pltpu.make_async_copy(a, b, in_sem.at[n])
        for n, (a, b) in enumerate(
            (
                (source_ref, source_in), (walker_ref, walker_in), (green_ref, green_in),
                (index_ref, index_in), (noise_ref, noise_in), (mean_ref, mean_in),
            )
        )
    ]
    for load in loads:
        load.start()
    own_h = pltpu.make_async_copy(
        half_ref.at[:, :, pl.ds(pl.multiple_of(chip * 128, 128), 128)],
        hrg.at[chip, :, pl.ds(0, 112)],
        misc.at[1],
    )
    own_h.start()
    own_l = pltpu.make_async_copy(
        chol_ref.at[:, :, core], lst.at[pl.ds(2 * core, 2)], misc.at[0]
    )
    own_l.start()

    hrg[:, :, 112:128, :] = jnp.zeros((8, 2, 16, 128), bf16)

    row8 = lax.broadcasted_iota(jnp.int32, (8, 128), 0)
    lane8 = lax.broadcasted_iota(jnp.int32, (8, 128), 1)
    loads[0].wait()
    lane1 = lax.broadcasted_iota(jnp.int32, (1, 128), 1)
    ids = jnp.zeros((1, 128), jnp.int32)
    for s in range(8):
        value = source_in[s]
        ids = jnp.where(lane1 == s, (value // 8) * 16 + value % 8, ids)
    stile[...] = ids.astype(f32)
    sall[walk] = ids.astype(f32)

    loads[1].wait()
    final[...] = jnp.zeros_like(final)
    final[:, 0:OCC] = walker_in[...].astype(f32).reshape(512, OCC)
    for p in range(WALK):
        zsend[p] = jnp.concatenate(
            [final[pl.ds(2 * p, 8, stride=64), :], final[pl.ds(2 * p + 1, 8, stride=64), :]],
            axis=0,
        ).astype(bf16)
    zrecv[walk] = zsend[walk]
    loads[2].wait()
    gp[:, core] = jnp.zeros((8, 64, 128), bf16)
    gp[:, core, :, 0:OCC] = green_in[...]

    pl.semaphore_wait(barrier, 15 + WALK - 1)

    def remote(src, dst, ssem, rsem, dev):
        return pltpu.make_async_remote_copy(
            src_ref=src, dst_ref=dst, send_sem=ssem, recv_sem=rsem,
            device_id=dev, device_id_type=MESH,
        )

    def chip_to(dz, dx):
        return ((z + dz) % 2) * 4 + (x + dx) % 4

    def chip_from(dz, dx):
        return ((z + dz) % 2) * 4 + (x + 4 - dx) % 4

    def walk_peer(d, sending):
        return (walk + d) % WALK if sending else (walk + WALK - d) % WALK

    def walk_copy(src, dst, ssem, rsem, d, sending):
        there = walk_peer(d, sending)
        return remote(src, dst, ssem.at[d], rsem.at[d], {"walk": there})

    def s_copy(d, sending):
        slot = walk if sending else walk_peer(d, sending)
        return walk_copy(stile, sall.at[slot], w_s, w_r, d, sending)

    def z_copy(d, sending):
        there = walk_peer(d, sending)
        slot = walk if sending else there
        return walk_copy(zsend.at[there], zrecv.at[slot], z_s, z_r, d, sending)

    def y_copy(d, sending):
        there = walk_peer(d, sending)
        slot = walk if sending else there
        return walk_copy(ysend.at[there], yrecv.at[slot], y_s, y_r, d, sending)

    def f_copy(d, sending):
        slot = walk if sending else walk_peer(d, sending)
        ref = fall.at[pl.ds(pl.multiple_of(8 * slot, 8), 8)]
        return walk_copy(ref, ref, f_s, f_r, d, sending)

    @pl.loop(1, WALK)
    def _(d):
        z_copy(d, True).start()
        s_copy(d, True).start()

    g_copy = remote(gp.at[:, core], gp.at[:, core], misc.at[2], misc.at[3], dev_sib)
    g_copy.start()
    g_got = remote(gp.at[:, 1 - core], gp.at[:, 1 - core], misc.at[2], misc.at[3], dev_sib)

    def hr_copy(k):
        there = chip_to(*OTHERS[k])
        return remote(
            half_ref.at[:, :, pl.ds(pl.multiple_of(there * 128, 128), 128)],
            hrg.at[chip, :, pl.ds(0, 112)],
            hr_s.at[k], hr_r.at[k], {"chol": there * 2 + core},
        )

    def hr_got(k):
        ref = hrg.at[chip_from(*OTHERS[k]), :, pl.ds(0, 112)]
        return remote(ref, ref, hr_s.at[k], hr_r.at[k], dev_sib)

    for k in range(7):
        hr_copy(k).start()

    l_copy = remote(
        chol_ref.at[:, :, 1 - core], lst.at[pl.ds(2 * core, 2)], misc.at[4], misc.at[5], dev_sib
    )
    l_got = remote(
        lst.at[pl.ds(2 * (1 - core), 2)], lst.at[pl.ds(2 * (1 - core), 2)],
        misc.at[4], misc.at[5], dev_sib,
    )

    def tiles(j):
        return pl.ds(SPANS[j][0], SPANS[j][1])

    def ag_send(ph, xg, j, k):
        ref = xg.at[tiles(j), chol]
        return remote(
            ref, ref, ag_s.at[ph, j, k], ag_r.at[ph, j, k],
            {"chol": chip_to(*OTHERS[k]) * 2 + core},
        )

    def ag_got(ph, xg, j, k):
        ref = xg.at[tiles(j), chip_from(*OTHERS[k]) * 2 + core]
        return remote(ref, ref, ag_s.at[ph, j, k], ag_r.at[ph, j, k], dev_sib)

    def sib(ph, xg, j, k, cc):
        there = chip if k == 7 else chip_from(*OTHERS[k])
        ref = xg.at[tiles(j), there * 2 + cc]
        return remote(ref, ref, sib_s.at[ph, j, k], sib_r.at[ph, j, k], dev_sib)

    def ag_start(ph, xg, j):
        for k in range(7):
            ag_send(ph, xg, j, k).start()
        sib(ph, xg, j, 7, core).start()

    def ag_relay(ph, xg, j):
        for k in reversed(range(7)):
            ag_got(ph, xg, j, k).wait_recv()
            sib(ph, xg, j, k, core).start()

    def ag_fin(ph, xg, j):
        for k in range(8):
            sib(ph, xg, j, k, 1 - core).wait_recv()

    def rs_copy(ph, j, k):
        there = chip_to(*OTHERS[k])
        return remote(
            part.at[ph, there, tiles(j)], got.at[ph, k, tiles(j)],
            rs_s.at[ph, j, k], rs_r.at[ph, j, k], {"chol": there * 2 + core},
        )

    def rs_start(ph, j):
        for k in range(7):
            rs_copy(ph, j, k).start()

    def rs_fin(ph, j):
        for k in range(7):
            rs_copy(ph, j, k).wait_recv()
        total = part[ph, chip, tiles(j)].astype(f32)
        for k in range(7):
            total = total + got[ph, k, tiles(j)].astype(f32)
        return total

    def matmul(ph, xg, j):
        start, size = SPANS[j]
        both = jnp.concatenate(
            [xg[start + n].reshape(1024, 128) for n in range(size)], axis=1
        )
        columns = pl.ds(0, 128 * size)
        for g in range(4):
            product = jnp.dot(
                lst[g].reshape(512, 1024), both, preferred_element_type=f32
            )
            scale = jnp.concatenate(
                [fb[g, pl.ds(start + n, 1), :] for n in range(size)], axis=1
            )
            if g == 0:
                acc[:, columns] = product * scale
            else:
                acc[:, columns] += product * scale
        for q in range(8):
            for n in range(size):
                part[ph, q, start + n] = acc[
                    pl.ds(64 * q, 64), pl.ds(128 * n, 128)
                ].astype(bf16)

    l_copy.start()

    @pl.loop(1, WALK)
    def _(d):
        s_copy(d, False).wait_recv()

    low = jnp.sum(
        jnp.where((lane8 == row8)[None], sall[...], 0.0), axis=2, keepdims=True
    )
    low = jnp.broadcast_to(low, (WALK, 8, 128))
    wanted = jnp.stack([low, low + 8], axis=1).reshape(WALK * 16, 128)
    wide = lax.broadcasted_iota(jnp.int32, (WALK * 16, 128), 1).astype(f32)
    picks = [jnp.where(wanted == wide + 128 * b, 1.0, 0.0).astype(bf16) for b in range(4)]

    @pl.loop(1, WALK)
    def _(d):
        z_copy(d, False).wait_recv()

    here = zrecv[...].reshape(WALK * 16, 128)
    taken = jnp.dot(picks[0], here[0:128], preferred_element_type=f32)
    for b in range(1, 4):
        taken = taken + jnp.dot(
            picks[b], here[128 * b : 128 * (b + 1)], preferred_element_type=f32
        )
    ysend[...] = taken.astype(bf16).reshape(WALK, 16, 128)
    yrecv[walk] = ysend[walk]

    @pl.loop(1, WALK)
    def _(d):
        y_copy(d, True).start()

    for load in loads[3:]:
        load.wait()
    own_h.wait()
    g_got.wait_recv()
    for k in range(7):
        hr_got(k).wait_recv()

    same = (
        lax.broadcasted_iota(jnp.int32, (64, 128), 0)
        == lax.broadcasted_iota(jnp.int32, (64, 128), 1) % 64
    ).astype(f32)

    def one_source(source, tile):
        pair = (hrg[source, 0], hrg[source, 1])
        picked = jnp.zeros((8, 128), f32)
        for half in range(2):
            columns = jnp.concatenate([h[:, 64 * half : 64 * half + 64] for h in pair], axis=1)
            product = jnp.dot(
                gp[:, half].reshape(512, 128), columns, preferred_element_type=f32
            )
            picked = picked + jnp.sum(product.reshape(8, 64, 128) * same[None], axis=1)
        for which in range(2):
            value = jnp.sum(
                jnp.where((lane8 >= 64) == bool(which), picked, 0.0), axis=1, keepdims=True
            )
            tile = jnp.where(
                lane8 == source * 4 + core * 2 + which, field_scale * value, tile
            )
        return tile

    tile = lax.fori_loop(0, 8, one_source, jnp.zeros((8, 128), f32))
    for which in range(2):
        shift = mean_in[index_in[which]]
        for w in range(8):
            tile = tile + jnp.where(
                (row8 == w) & (lane8 == chol * 2 + which),
                noise_in[which, w] - field_scale * shift, 0.0,
            )
    btile[chol] = tile

    def b_copy(d, sending):
        there = (chol + d) % 16 if sending else (chol + 16 - d) % 16
        slot = chol if sending else there
        return remote(
            btile.at[slot], btile.at[slot], b_s.at[d], b_r.at[d], {"chol": there}
        )

    @pl.loop(1, 16)
    def _(d):
        b_copy(d, True).start()

    @pl.loop(1, WALK)
    def _(d):
        y_copy(d, False).wait_recv()

    for p in range(WALK):
        both = yrecv[p].astype(f32)
        final[pl.ds(2 * p, 8, stride=64), :] = both[0:8]
        final[pl.ds(2 * p + 1, 8, stride=64), :] = both[8:16]
    lanes = lax.broadcasted_iota(jnp.int32, (64, 128), 1)
    shifted = [final[pl.ds(64 * w, 64)] for w in range(8)]
    shifted = [
        pltpu.roll(v, (OCC * w) % 128, 1) if w else v for w, v in enumerate(shifted)
    ]
    for t in range(TILES):
        tile = jnp.zeros((64, 128), f32)
        for w in range(8):
            left, right = OCC * w - 128 * t, OCC * (w + 1) - 128 * t
            if right > 0 and left < 128:
                tile = jnp.where((lanes >= left) & (lanes < right), shifted[w], tile)
        xg1[t, chol] = tile.astype(bf16)
    for j in range(CHUNKS):
        ag_start(0, xg1, j)

    @pl.loop(1, 16)
    def _(d):
        b_copy(d, False).wait_recv()

    field = btile[0]
    for c in range(1, 16):
        field = field + btile[c]
    fall[pl.ds(pl.multiple_of(8 * walk, 8), 8)] = field

    @pl.loop(1, WALK)
    def _(d):
        f_copy(d, True).start()

    ag_relay(0, xg1, 0)

    @pl.loop(1, WALK)
    def _(d):
        f_copy(d, False).wait_recv()

    for s in range(8):
        fsel[pl.ds(s, 1), :] = fall[pl.ds(source_in[s], 1), :]
    field = fsel[...]
    for g in range(4):
        value = jnp.sum(
            jnp.where(lane8 == chip * 4 + g, field, 0.0), axis=1, keepdims=True
        )
        for t in range(TILES):
            column = lane8 + 128 * t
            mine = (column >= OCC * row8) & (column < OCC * (row8 + 1))
            fb[g, pl.ds(t, 1), :] = jnp.sum(
                jnp.where(mine, value, 0.0), axis=0, keepdims=True
            )

    ag_relay(0, xg1, 1)
    own_l.wait()
    l_got.wait_recv()

    def mm1(j):
        ag_fin(0, xg1, j)
        matmul(0, xg1, j)
        rs_start(0, j)

    def turn(j):
        term = field_scale * rs_fin(0, j)
        first[tiles(j)] = term
        xg2[tiles(j), chol] = term.astype(bf16)
        ag_start(1, xg2, j)

    def mm2(j):
        ag_fin(1, xg2, j)
        matmul(1, xg2, j)
        rs_start(1, j)

    def finish(j):
        done_tiles = (
            xg1[tiles(j), chol].astype(f32)
            + first[tiles(j)]
            + (0.5 * field_scale) * rs_fin(1, j)
        )
        first[tiles(j)] = done_tiles

    mm1(0)
    ag_relay(0, xg1, 2)
    mm1(1)
    ag_relay(0, xg1, 3)
    turn(0)
    mm1(2)
    turn(1)
    mm1(3)
    ag_relay(1, xg2, 0)
    turn(2)
    ag_relay(1, xg2, 1)
    mm2(0)
    turn(3)
    ag_relay(1, xg2, 2)
    mm2(1)
    ag_relay(1, xg2, 3)
    finish(0)
    mm2(2)
    finish(1)
    mm2(3)
    finish(2)
    finish(3)

    for w in range(8):
        t, start = (OCC * w) // 128, (OCC * w) % 128
        if start:
            mixed = jnp.where(lanes >= start, first[t], first[min(t + 1, TILES - 1)])
            mixed = pltpu.roll(mixed, 128 - start, 1)
        else:
            mixed = first[t]
        out_ref[w] = mixed[:, 0:OCC].astype(bf16)

    g_copy.wait_send()
    l_copy.wait_send()
    for k in range(7):
        hr_copy(k).wait_send()

    @pl.loop(1, 16)
    def _(d):
        b_copy(d, True).wait_send()

    for ph, xg in ((0, xg1), (1, xg2)):
        for j in range(CHUNKS):
            for k in range(7):
                ag_send(ph, xg, j, k).wait_send()
                rs_copy(ph, j, k).wait_send()
            for k in range(8):
                sib(ph, xg, j, k, core).wait_send()

    @pl.loop(1, WALK)
    def _(d):
        s_copy(d, True).wait_send()
        z_copy(d, True).wait_send()
        y_copy(d, True).wait_send()
        f_copy(d, True).wait_send()


def per_device(
    cholesky, half_rotated, green_half, walker, aux_noise, mf_shift, chol_index, walker_source
):
    bf16, f32, i32 = jnp.bfloat16, jnp.float32, jnp.int32
    V, S, D = pltpu.VMEM, pltpu.SMEM, pltpu.SemaphoreType.DMA
    moved = pl.pallas_call(
        body,
        out_shape=jax.ShapeDtypeStruct((8, 64, OCC), bf16),
        in_specs=[pl.BlockSpec(memory_space=pltpu.HBM)] * 8,
        out_specs=pl.BlockSpec(memory_space=pltpu.VMEM),
        scratch_shapes=[
            V((4, 8, 64, 1024), bf16),
            V((TILES, 16, 64, 128), bf16),
            V((TILES, 16, 64, 128), bf16),
            V((2, 8, TILES, 64, 128), bf16),
            V((2, 7, TILES, 64, 128), bf16),
            V((TILES, 64, 128), f32),
            V((512, 256), f32),
            V((8, 2, 128, 128), bf16),
            V((8, 2, 64, 128), bf16),
            V((4, 8, 128), f32),
            V((16, 8, 128), f32),
            V((512, 128), f32),
            V((WALK, 16, 128), bf16),
            V((WALK, 16, 128), bf16),
            V((WALK, 16, 128), bf16),
            V((WALK, 16, 128), bf16),
            V((1, 128), f32),
            V((WALK, 1, 128), f32),
            V((256, 128), f32),
            V((8, 128), f32),
            V((8, 64, OCC), bf16),
            V((8, 64, OCC), bf16),
            S((2, 8), f32),
            S((4000,), f32),
            S((2,), i32),
            S((8,), i32),
            D((2, CHUNKS, 7)),
            D((2, CHUNKS, 7)),
            D((2, CHUNKS, 8)),
            D((2, CHUNKS, 8)),
            D((2, CHUNKS, 7)),
            D((2, CHUNKS, 7)),
            D((7,)),
            D((7,)),
            D((16,)),
            D((16,)),
            D((WALK,)),
            D((WALK,)),
            D((WALK,)),
            D((WALK,)),
            D((WALK,)),
            D((WALK,)),
            D((WALK,)),
            D((WALK,)),
            D((6,)),
            D((6,)),
        ],
        compiler_params=pltpu.CompilerParams(
            collective_id=0, has_side_effects=True, vmem_limit_bytes=64 * 1024 * 1024
        ),
        cost_estimate=pl.CostEstimate(
            flops=8_600_000_000, bytes_accessed=6_000_000, transcendentals=0
        ),
    )(
        cholesky.reshape(2, 8, 2, 64, 1024),
        jnp.pad(half_rotated, ((0, 0), (0, 12), (0, 0))),
        jnp.transpose(green_half, (0, 2, 1)),
        jnp.transpose(walker, (0, 2, 1)),
        jnp.transpose(aux_noise, (1, 0)),
        mf_shift,
        chol_index,
        walker_source,
    )
    return jnp.transpose(moved, (0, 2, 1))


def solution(mesh):
    placed = (
        P("chol", None, None),
        P("chol", None, None),
        P("walk", None, "chol"),
        P("walk", None, "chol"),
        P("walk", "chol"),
        P(),
        P("chol"),
        P("walk"),
    )
    return jax.shard_map(
        per_device, mesh=mesh, in_specs=placed, out_specs=P("walk", None, "chol"), check_vma=False
    )
```

```python
import jax
import jax.numpy as jnp
from jax import lax
from jax.experimental import pallas as pl
from jax.experimental.pallas import tpu as pltpu
from jax.sharding import PartitionSpec as P

MESH = pl.DeviceIdType.MESH
field_scale = 0.1
TILES = 7
SPANS = ((0, 1), (1, 2), (3, 2), (5, 2))
CHUNKS = len(SPANS)
WALK = 32
OCC = 100
OTHERS = ((1, 2), (0, 2), (1, 1), (1, 3), (0, 1), (0, 3), (1, 0))


def body(
    chol_ref, half_ref, green_ref, walker_ref, noise_ref, mean_ref, index_ref, source_ref,
    out_ref,
    lst, xg1, xg2, part, got, first, acc, hrg, gp, fb, btile, final,
    zsend, zrecv, ysend, yrecv, stile, sall, fall, fsel,
    green_in, walker_in, noise_in, mean_in, index_in, source_in,
    ag_s, ag_r, sib_s, sib_r, rs_s, rs_r, hr_s, hr_r, b_s, b_r, w_s, w_r, z_s, z_r, y_s, y_r, f_s, f_r,
    misc, in_sem,
):
    f32, bf16 = jnp.float32, jnp.bfloat16
    walk = lax.axis_index("walk")
    chol = lax.axis_index("chol")
    core = chol % 2
    chip = chol // 2
    x, z = chip % 4, chip // 4
    dev_sib = {"chol": chip * 2 + 1 - core}

    barrier = pltpu.get_barrier_semaphore()

    @pl.loop(1, WALK)
    def _(d):
        pl.semaphore_signal(
            barrier, inc=1, device_id={"walk": (walk + d) % WALK}, device_id_type=MESH
        )

    @pl.loop(1, 16)
    def _(d):
        pl.semaphore_signal(
            barrier, inc=1, device_id={"chol": (chol + d) % 16}, device_id_type=MESH
        )

    loads = [
        pltpu.make_async_copy(a, b, in_sem.at[n])
        for n, (a, b) in enumerate(
            (
                (source_ref, source_in), (walker_ref, walker_in), (green_ref, green_in),
                (index_ref, index_in), (noise_ref, noise_in), (mean_ref, mean_in),
            )
        )
    ]
    for load in loads:
        load.start()
    own_h = pltpu.make_async_copy(
        half_ref.at[:, :, pl.ds(pl.multiple_of(chip * 128, 128), 128)],
        hrg.at[chip, :, pl.ds(0, 112)],
        misc.at[1],
    )
    own_h.start()
    own_l = pltpu.make_async_copy(
        chol_ref.at[:, :, core], lst.at[pl.ds(2 * core, 2)], misc.at[0]
    )
    own_l.start()

    hrg[:, :, 112:128, :] = jnp.zeros((8, 2, 16, 128), bf16)

    row8 = lax.broadcasted_iota(jnp.int32, (8, 128), 0)
    lane8 = lax.broadcasted_iota(jnp.int32, (8, 128), 1)
    loads[0].wait()
    lane1 = lax.broadcasted_iota(jnp.int32, (1, 128), 1)
    ids = jnp.zeros((1, 128), jnp.int32)
    for s in range(8):
        value = source_in[s]
        ids = jnp.where(lane1 == s, (value // 8) * 16 + value % 8, ids)
    stile[...] = ids.astype(f32)
    sall[walk] = ids.astype(f32)

    loads[1].wait()
    final[...] = jnp.zeros_like(final)
    final[:, 0:OCC] = walker_in[...].astype(f32).reshape(512, OCC)
    for p in range(WALK):
        zsend[p] = jnp.concatenate(
            [final[pl.ds(2 * p, 8, stride=64), :], final[pl.ds(2 * p + 1, 8, stride=64), :]],
            axis=0,
        ).astype(bf16)
    zrecv[walk] = zsend[walk]
    loads[2].wait()
    gp[:, core] = jnp.zeros((8, 64, 128), bf16)
    gp[:, core, :, 0:OCC] = green_in[...]

    pl.semaphore_wait(barrier, 15 + WALK - 1)

    def remote(src, dst, ssem, rsem, dev):
        return pltpu.make_async_remote_copy(
            src_ref=src, dst_ref=dst, send_sem=ssem, recv_sem=rsem,
            device_id=dev, device_id_type=MESH,
        )

    def chip_to(dz, dx):
        return ((z + dz) % 2) * 4 + (x + dx) % 4

    def chip_from(dz, dx):
        return ((z + dz) % 2) * 4 + (x + 4 - dx) % 4

    def walk_peer(d, sending):
        return (walk + d) % WALK if sending else (walk + WALK - d) % WALK

    def walk_copy(src, dst, ssem, rsem, d, sending):
        there = walk_peer(d, sending)
        return remote(src, dst, ssem.at[d], rsem.at[d], {"walk": there})

    def s_copy(d, sending):
        slot = walk if sending else walk_peer(d, sending)
        return walk_copy(stile, sall.at[slot], w_s, w_r, d, sending)

    def z_copy(d, sending):
        there = walk_peer(d, sending)
        slot = walk if sending else there
        return walk_copy(zsend.at[there], zrecv.at[slot], z_s, z_r, d, sending)

    def y_copy(d, sending):
        there = walk_peer(d, sending)
        slot = walk if sending else there
        return walk_copy(ysend.at[there], yrecv.at[slot], y_s, y_r, d, sending)

    def f_copy(d, sending):
        slot = walk if sending else walk_peer(d, sending)
        ref = fall.at[pl.ds(pl.multiple_of(8 * slot, 8), 8)]
        return walk_copy(ref, ref, f_s, f_r, d, sending)

    @pl.loop(1, WALK)
    def _(d):
        z_copy(d, True).start()
        s_copy(d, True).start()

    g_copy = remote(gp.at[:, core], gp.at[:, core], misc.at[2], misc.at[3], dev_sib)
    g_copy.start()
    g_got = remote(gp.at[:, 1 - core], gp.at[:, 1 - core], misc.at[2], misc.at[3], dev_sib)

    def hr_copy(k):
        there = chip_to(*OTHERS[k])
        return remote(
            half_ref.at[:, :, pl.ds(pl.multiple_of(there * 128, 128), 128)],
            hrg.at[chip, :, pl.ds(0, 112)],
            hr_s.at[k], hr_r.at[k], {"chol": there * 2 + core},
        )

    def hr_got(k):
        ref = hrg.at[chip_from(*OTHERS[k]), :, pl.ds(0, 112)]
        return remote(ref, ref, hr_s.at[k], hr_r.at[k], dev_sib)

    for k in range(7):
        hr_copy(k).start()

    l_copy = remote(
        chol_ref.at[:, :, 1 - core], lst.at[pl.ds(2 * core, 2)], misc.at[4], misc.at[5], dev_sib
    )
    l_got = remote(
        lst.at[pl.ds(2 * (1 - core), 2)], lst.at[pl.ds(2 * (1 - core), 2)],
        misc.at[4], misc.at[5], dev_sib,
    )

    def tiles(j):
        return pl.ds(SPANS[j][0], SPANS[j][1])

    def ag_send(ph, xg, j, k):
        ref = xg.at[tiles(j), chol]
        return remote(
            ref, ref, ag_s.at[ph, j, k], ag_r.at[ph, j, k],
            {"chol": chip_to(*OTHERS[k]) * 2 + core},
        )

    def ag_got(ph, xg, j, k):
        ref = xg.at[tiles(j), chip_from(*OTHERS[k]) * 2 + core]
        return remote(ref, ref, ag_s.at[ph, j, k], ag_r.at[ph, j, k], dev_sib)

    def sib(ph, xg, j, k, cc):
        there = chip if k == 7 else chip_from(*OTHERS[k])
        ref = xg.at[tiles(j), there * 2 + cc]
        return remote(ref, ref, sib_s.at[ph, j, k], sib_r.at[ph, j, k], dev_sib)

    def ag_start(ph, xg, j):
        for k in range(7):
            ag_send(ph, xg, j, k).start()
        sib(ph, xg, j, 7, core).start()

    def ag_relay(ph, xg, j):
        for k in reversed(range(7)):
            ag_got(ph, xg, j, k).wait_recv()
            sib(ph, xg, j, k, core).start()

    def ag_fin(ph, xg, j):
        for k in range(8):
            sib(ph, xg, j, k, 1 - core).wait_recv()

    def rs_copy(ph, j, k):
        there = chip_to(*OTHERS[k])
        return remote(
            part.at[ph, there, tiles(j)], got.at[ph, k, tiles(j)],
            rs_s.at[ph, j, k], rs_r.at[ph, j, k], {"chol": there * 2 + core},
        )

    def rs_start(ph, j):
        for k in range(7):
            rs_copy(ph, j, k).start()

    def rs_fin(ph, j):
        for k in range(7):
            rs_copy(ph, j, k).wait_recv()
        total = part[ph, chip, tiles(j)].astype(f32)
        for k in range(7):
            total = total + got[ph, k, tiles(j)].astype(f32)
        return total

    def matmul(ph, xg, j):
        start, size = SPANS[j]
        both = jnp.concatenate(
            [xg[start + n].reshape(1024, 128) for n in range(size)], axis=1
        )
        columns = pl.ds(0, 128 * size)
        for g in range(4):
            product = jnp.dot(
                lst[g].reshape(512, 1024), both, preferred_element_type=f32
            )
            scale = jnp.concatenate(
                [fb[g, pl.ds(start + n, 1), :] for n in range(size)], axis=1
            )
            if g == 0:
                acc[:, columns] = product * scale
            else:
                acc[:, columns] += product * scale
        for q in range(8):
            for n in range(size):
                part[ph, q, start + n] = acc[
                    pl.ds(64 * q, 64), pl.ds(128 * n, 128)
                ].astype(bf16)

    l_copy.start()

    @pl.loop(1, WALK)
    def _(d):
        s_copy(d, False).wait_recv()

    low = jnp.sum(
        jnp.where((lane8 == row8)[None], sall[...], 0.0), axis=2, keepdims=True
    )
    low = jnp.broadcast_to(low, (WALK, 8, 128))
    wanted = jnp.stack([low, low + 8], axis=1).reshape(WALK * 16, 128)
    wide = lax.broadcasted_iota(jnp.int32, (WALK * 16, 128), 1).astype(f32)
    picks = [jnp.where(wanted == wide + 128 * b, 1.0, 0.0).astype(bf16) for b in range(4)]

    @pl.loop(1, WALK)
    def _(d):
        z_copy(d, False).wait_recv()

    here = zrecv[...].reshape(WALK * 16, 128)
    taken = jnp.dot(picks[0], here[0:128], preferred_element_type=f32)
    for b in range(1, 4):
        taken = taken + jnp.dot(
            picks[b], here[128 * b : 128 * (b + 1)], preferred_element_type=f32
        )
    ysend[...] = taken.astype(bf16).reshape(WALK, 16, 128)
    yrecv[walk] = ysend[walk]

    @pl.loop(1, WALK)
    def _(d):
        y_copy(d, True).start()

    for load in loads[3:]:
        load.wait()
    own_h.wait()
    g_got.wait_recv()
    for k in range(7):
        hr_got(k).wait_recv()

    same = (
        lax.broadcasted_iota(jnp.int32, (64, 128), 0)
        == lax.broadcasted_iota(jnp.int32, (64, 128), 1) % 64
    ).astype(f32)

    def one_source(source, tile):
        pair = (hrg[source, 0], hrg[source, 1])
        picked = jnp.zeros((8, 128), f32)
        for half in range(2):
            columns = jnp.concatenate([h[:, 64 * half : 64 * half + 64] for h in pair], axis=1)
            product = jnp.dot(
                gp[:, half].reshape(512, 128), columns, preferred_element_type=f32
            )
            picked = picked + jnp.sum(product.reshape(8, 64, 128) * same[None], axis=1)
        for which in range(2):
            value = jnp.sum(
                jnp.where((lane8 >= 64) == bool(which), picked, 0.0), axis=1, keepdims=True
            )
            tile = jnp.where(
                lane8 == source * 4 + core * 2 + which, field_scale * value, tile
            )
        return tile

    tile = lax.fori_loop(0, 8, one_source, jnp.zeros((8, 128), f32))
    for which in range(2):
        shift = mean_in[index_in[which]]
        for w in range(8):
            tile = tile + jnp.where(
                (row8 == w) & (lane8 == chol * 2 + which),
                noise_in[which, w] - field_scale * shift, 0.0,
            )
    btile[chol] = tile

    def b_copy(d, sending):
        there = (chol + d) % 16 if sending else (chol + 16 - d) % 16
        slot = chol if sending else there
        return remote(
            btile.at[slot], btile.at[slot], b_s.at[d], b_r.at[d], {"chol": there}
        )

    @pl.loop(1, 16)
    def _(d):
        b_copy(d, True).start()

    @pl.loop(1, WALK)
    def _(d):
        y_copy(d, False).wait_recv()

    for p in range(WALK):
        both = yrecv[p].astype(f32)
        final[pl.ds(2 * p, 8, stride=64), :] = both[0:8]
        final[pl.ds(2 * p + 1, 8, stride=64), :] = both[8:16]
    lanes = lax.broadcasted_iota(jnp.int32, (64, 128), 1)
    shifted = [final[pl.ds(64 * w, 64)] for w in range(8)]
    shifted = [
        pltpu.roll(v, (OCC * w) % 128, 1) if w else v for w, v in enumerate(shifted)
    ]
    for t in range(TILES):
        tile = jnp.zeros((64, 128), f32)
        for w in range(8):
            left, right = OCC * w - 128 * t, OCC * (w + 1) - 128 * t
            if right > 0 and left < 128:
                tile = jnp.where((lanes >= left) & (lanes < right), shifted[w], tile)
        xg1[t, chol] = tile.astype(bf16)
    ag_start(0, xg1, 0)
    ag_start(0, xg1, 1)

    @pl.loop(1, 16)
    def _(d):
        b_copy(d, False).wait_recv()

    field = btile[0]
    for c in range(1, 16):
        field = field + btile[c]
    fall[pl.ds(pl.multiple_of(8 * walk, 8), 8)] = field

    @pl.loop(1, WALK)
    def _(d):
        f_copy(d, True).start()

    ag_relay(0, xg1, 0)
    ag_start(0, xg1, 2)

    @pl.loop(1, WALK)
    def _(d):
        f_copy(d, False).wait_recv()

    for s in range(8):
        fsel[pl.ds(s, 1), :] = fall[pl.ds(source_in[s], 1), :]
    field = fsel[...]
    for g in range(4):
        value = jnp.sum(
            jnp.where(lane8 == chip * 4 + g, field, 0.0), axis=1, keepdims=True
        )
        for t in range(TILES):
            column = lane8 + 128 * t
            mine = (column >= OCC * row8) & (column < OCC * (row8 + 1))
            fb[g, pl.ds(t, 1), :] = jnp.sum(
                jnp.where(mine, value, 0.0), axis=0, keepdims=True
            )

    ag_relay(0, xg1, 1)
    ag_start(0, xg1, 3)
    own_l.wait()
    l_got.wait_recv()

    def mm1(j):
        ag_fin(0, xg1, j)
        matmul(0, xg1, j)
        rs_start(0, j)

    def turn(j):
        term = field_scale * rs_fin(0, j)
        first[tiles(j)] = term
        xg2[tiles(j), chol] = term.astype(bf16)
        ag_start(1, xg2, j)

    def mm2(j):
        ag_fin(1, xg2, j)
        matmul(1, xg2, j)
        rs_start(1, j)

    def finish(j):
        done_tiles = (
            xg1[tiles(j), chol].astype(f32)
            + first[tiles(j)]
            + (0.5 * field_scale) * rs_fin(1, j)
        )
        first[tiles(j)] = done_tiles

    mm1(0)
    ag_relay(0, xg1, 2)
    mm1(1)
    ag_relay(0, xg1, 3)
    turn(0)
    mm1(2)
    turn(1)
    mm1(3)
    ag_relay(1, xg2, 0)
    turn(2)
    ag_relay(1, xg2, 1)
    mm2(0)
    turn(3)
    ag_relay(1, xg2, 2)
    mm2(1)
    ag_relay(1, xg2, 3)
    finish(0)
    mm2(2)
    finish(1)
    mm2(3)
    finish(2)
    finish(3)

    for w in range(8):
        t, start = (OCC * w) // 128, (OCC * w) % 128
        if start:
            mixed = jnp.where(lanes >= start, first[t], first[min(t + 1, TILES - 1)])
            mixed = pltpu.roll(mixed, 128 - start, 1)
        else:
            mixed = first[t]
        out_ref[w] = mixed[:, 0:OCC].astype(bf16)

    g_copy.wait_send()
    l_copy.wait_send()
    for k in range(7):
        hr_copy(k).wait_send()

    @pl.loop(1, 16)
    def _(d):
        b_copy(d, True).wait_send()

    for ph, xg in ((0, xg1), (1, xg2)):
        for j in range(CHUNKS):
            for k in range(7):
                ag_send(ph, xg, j, k).wait_send()
                rs_copy(ph, j, k).wait_send()
            for k in range(8):
                sib(ph, xg, j, k, core).wait_send()

    @pl.loop(1, WALK)
    def _(d):
        s_copy(d, True).wait_send()
        z_copy(d, True).wait_send()
        y_copy(d, True).wait_send()
        f_copy(d, True).wait_send()


def per_device(
    cholesky, half_rotated, green_half, walker, aux_noise, mf_shift, chol_index, walker_source
):
    bf16, f32, i32 = jnp.bfloat16, jnp.float32, jnp.int32
    V, S, D = pltpu.VMEM, pltpu.SMEM, pltpu.SemaphoreType.DMA
    moved = pl.pallas_call(
        body,
        out_shape=jax.ShapeDtypeStruct((8, 64, OCC), bf16),
        in_specs=[pl.BlockSpec(memory_space=pltpu.HBM)] * 8,
        out_specs=pl.BlockSpec(memory_space=pltpu.VMEM),
        scratch_shapes=[
            V((4, 8, 64, 1024), bf16),
            V((TILES, 16, 64, 128), bf16),
            V((TILES, 16, 64, 128), bf16),
            V((2, 8, TILES, 64, 128), bf16),
            V((2, 7, TILES, 64, 128), bf16),
            V((TILES, 64, 128), f32),
            V((512, 256), f32),
            V((8, 2, 128, 128), bf16),
            V((8, 2, 64, 128), bf16),
            V((4, 8, 128), f32),
            V((16, 8, 128), f32),
            V((512, 128), f32),
            V((WALK, 16, 128), bf16),
            V((WALK, 16, 128), bf16),
            V((WALK, 16, 128), bf16),
            V((WALK, 16, 128), bf16),
            V((1, 128), f32),
            V((WALK, 1, 128), f32),
            V((256, 128), f32),
            V((8, 128), f32),
            V((8, 64, OCC), bf16),
            V((8, 64, OCC), bf16),
            S((2, 8), f32),
            S((4000,), f32),
            S((2,), i32),
            S((8,), i32),
            D((2, CHUNKS, 7)),
            D((2, CHUNKS, 7)),
            D((2, CHUNKS, 8)),
            D((2, CHUNKS, 8)),
            D((2, CHUNKS, 7)),
            D((2, CHUNKS, 7)),
            D((7,)),
            D((7,)),
            D((16,)),
            D((16,)),
            D((WALK,)),
            D((WALK,)),
            D((WALK,)),
            D((WALK,)),
            D((WALK,)),
            D((WALK,)),
            D((WALK,)),
            D((WALK,)),
            D((6,)),
            D((6,)),
        ],
        compiler_params=pltpu.CompilerParams(
            collective_id=0, has_side_effects=True, vmem_limit_bytes=64 * 1024 * 1024
        ),
        cost_estimate=pl.CostEstimate(
            flops=8_600_000_000, bytes_accessed=6_000_000, transcendentals=0
        ),
    )(
        cholesky.reshape(2, 8, 2, 64, 1024),
        jnp.pad(half_rotated, ((0, 0), (0, 12), (0, 0))),
        jnp.transpose(green_half, (0, 2, 1)),
        jnp.transpose(walker, (0, 2, 1)),
        jnp.transpose(aux_noise, (1, 0)),
        mf_shift,
        chol_index,
        walker_source,
    )
    return jnp.transpose(moved, (0, 2, 1))


def solution(mesh):
    placed = (
        P("chol", None, None),
        P("chol", None, None),
        P("walk", None, "chol"),
        P("walk", None, "chol"),
        P("walk", "chol"),
        P(),
        P("chol"),
        P("walk"),
    )
    return jax.shard_map(
        per_device, mesh=mesh, in_specs=placed, out_specs=P("walk", None, "chol"), check_vma=False
    )
```

```python
import jax
import jax.numpy as jnp
from jax import lax
from jax.experimental import pallas as pl
from jax.experimental.pallas import tpu as pltpu
from jax.sharding import PartitionSpec as P

MESH = pl.DeviceIdType.MESH
field_scale = 0.1
TILES = 7
SPANS = ((0, 1), (1, 2), (3, 2), (5, 2))
CHUNKS = len(SPANS)
WALK = 32
OCC = 100
OTHERS = ((1, 2), (0, 2), (1, 1), (1, 3), (0, 1), (0, 3), (1, 0))


def body(
    chol_ref, half_ref, green_ref, walker_ref, noise_ref, mean_ref, index_ref, source_ref,
    out_ref,
    lst, xg1, xg2, part, got, first, acc, hrg, gp, fb, btile, final,
    zsend, zrecv, ysend, yrecv, stile, sall, fall, fsel,
    green_in, walker_in, noise_in, mean_in, index_in, source_in,
    ag_s, ag_r, sib_s, sib_r, rs_s, rs_r, hr_s, hr_r, b_s, b_r, w_s, w_r, z_s, z_r, y_s, y_r, f_s, f_r,
    misc, in_sem,
):
    f32, bf16 = jnp.float32, jnp.bfloat16
    walk = lax.axis_index("walk")
    chol = lax.axis_index("chol")
    core = chol % 2
    chip = chol // 2
    x, z = chip % 4, chip // 4
    dev_sib = {"chol": chip * 2 + 1 - core}

    barrier = pltpu.get_barrier_semaphore()

    @pl.loop(1, WALK)
    def _(d):
        pl.semaphore_signal(
            barrier, inc=1, device_id={"walk": (walk + d) % WALK}, device_id_type=MESH
        )

    @pl.loop(1, 16)
    def _(d):
        pl.semaphore_signal(
            barrier, inc=1, device_id={"chol": (chol + d) % 16}, device_id_type=MESH
        )

    loads = [
        pltpu.make_async_copy(a, b, in_sem.at[n])
        for n, (a, b) in enumerate(
            (
                (source_ref, source_in), (walker_ref, walker_in), (green_ref, green_in),
                (index_ref, index_in), (noise_ref, noise_in), (mean_ref, mean_in),
            )
        )
    ]
    for load in loads:
        load.start()
    own_h = pltpu.make_async_copy(
        half_ref.at[:, :, pl.ds(pl.multiple_of(chip * 128, 128), 128)],
        hrg.at[chip, :, pl.ds(0, 112)],
        misc.at[1],
    )
    own_h.start()
    own_l = pltpu.make_async_copy(
        chol_ref.at[:, :, core], lst.at[pl.ds(2 * core, 2)], misc.at[0]
    )
    own_l.start()

    hrg[:, :, 112:128, :] = jnp.zeros((8, 2, 16, 128), bf16)

    row8 = lax.broadcasted_iota(jnp.int32, (8, 128), 0)
    lane8 = lax.broadcasted_iota(jnp.int32, (8, 128), 1)
    loads[0].wait()
    lane1 = lax.broadcasted_iota(jnp.int32, (1, 128), 1)
    ids = jnp.zeros((1, 128), jnp.int32)
    for s in range(8):
        value = source_in[s]
        ids = jnp.where(lane1 == s, (value // 8) * 16 + value % 8, ids)
    stile[...] = ids.astype(f32)
    sall[walk] = ids.astype(f32)

    loads[1].wait()
    final[...] = jnp.zeros_like(final)
    final[:, 0:OCC] = walker_in[...].astype(f32).reshape(512, OCC)
    for p in range(WALK):
        zsend[p] = jnp.concatenate(
            [final[pl.ds(2 * p, 8, stride=64), :], final[pl.ds(2 * p + 1, 8, stride=64), :]],
            axis=0,
        ).astype(bf16)
    zrecv[walk] = zsend[walk]
    loads[2].wait()
    gp[:, core] = jnp.zeros((8, 64, 128), bf16)
    gp[:, core, :, 0:OCC] = green_in[...]

    pl.semaphore_wait(barrier, 15 + WALK - 1)

    def remote(src, dst, ssem, rsem, dev):
        return pltpu.make_async_remote_copy(
            src_ref=src, dst_ref=dst, send_sem=ssem, recv_sem=rsem,
            device_id=dev, device_id_type=MESH,
        )

    def chip_to(dz, dx):
        return ((z + dz) % 2) * 4 + (x + dx) % 4

    def chip_from(dz, dx):
        return ((z + dz) % 2) * 4 + (x + 4 - dx) % 4

    def walk_peer(d, sending):
        return (walk + d) % WALK if sending else (walk + WALK - d) % WALK

    def walk_copy(src, dst, ssem, rsem, d, sending):
        there = walk_peer(d, sending)
        return remote(src, dst, ssem.at[d], rsem.at[d], {"walk": there})

    def s_copy(d, sending):
        slot = walk if sending else walk_peer(d, sending)
        return walk_copy(stile, sall.at[slot], w_s, w_r, d, sending)

    def z_copy(d, sending):
        there = walk_peer(d, sending)
        slot = walk if sending else there
        return walk_copy(zsend.at[there], zrecv.at[slot], z_s, z_r, d, sending)

    def y_copy(d, sending):
        there = walk_peer(d, sending)
        slot = walk if sending else there
        return walk_copy(ysend.at[there], yrecv.at[slot], y_s, y_r, d, sending)

    def f_copy(d, sending):
        slot = walk if sending else walk_peer(d, sending)
        ref = fall.at[pl.ds(pl.multiple_of(8 * slot, 8), 8)]
        return walk_copy(ref, ref, f_s, f_r, d, sending)

    @pl.loop(1, WALK)
    def _(d):
        z_copy(d, True).start()
        s_copy(d, True).start()

    g_copy = remote(gp.at[:, core], gp.at[:, core], misc.at[2], misc.at[3], dev_sib)
    g_copy.start()
    g_got = remote(gp.at[:, 1 - core], gp.at[:, 1 - core], misc.at[2], misc.at[3], dev_sib)

    def hr_copy(k):
        there = chip_to(*OTHERS[k])
        return remote(
            half_ref.at[:, :, pl.ds(pl.multiple_of(there * 128, 128), 128)],
            hrg.at[chip, :, pl.ds(0, 112)],
            hr_s.at[k], hr_r.at[k], {"chol": there * 2 + core},
        )

    def hr_got(k):
        ref = hrg.at[chip_from(*OTHERS[k]), :, pl.ds(0, 112)]
        return remote(ref, ref, hr_s.at[k], hr_r.at[k], dev_sib)

    for k in range(7):
        hr_copy(k).start()

    l_copy = remote(
        chol_ref.at[:, :, 1 - core], lst.at[pl.ds(2 * core, 2)], misc.at[4], misc.at[5], dev_sib
    )
    l_got = remote(
        lst.at[pl.ds(2 * (1 - core), 2)], lst.at[pl.ds(2 * (1 - core), 2)],
        misc.at[4], misc.at[5], dev_sib,
    )

    def tiles(j):
        return pl.ds(SPANS[j][0], SPANS[j][1])

    def ag_send(ph, xg, j, k):
        ref = xg.at[tiles(j), chol]
        return remote(
            ref, ref, ag_s.at[ph, j, k], ag_r.at[ph, j, k],
            {"chol": chip_to(*OTHERS[k]) * 2 + core},
        )

    def ag_got(ph, xg, j, k):
        ref = xg.at[tiles(j), chip_from(*OTHERS[k]) * 2 + core]
        return remote(ref, ref, ag_s.at[ph, j, k], ag_r.at[ph, j, k], dev_sib)

    def sib(ph, xg, j, k, cc):
        there = chip if k == 7 else chip_from(*OTHERS[k])
        ref = xg.at[tiles(j), there * 2 + cc]
        return remote(ref, ref, sib_s.at[ph, j, k], sib_r.at[ph, j, k], dev_sib)

    def ag_start(ph, xg, j):
        for k in range(7):
            ag_send(ph, xg, j, k).start()
        sib(ph, xg, j, 7, core).start()

    def ag_relay(ph, xg, j):
        for k in reversed(range(7)):
            ag_got(ph, xg, j, k).wait_recv()
            sib(ph, xg, j, k, core).start()

    def ag_fin(ph, xg, j):
        for k in range(8):
            sib(ph, xg, j, k, 1 - core).wait_recv()

    def rs_copy(ph, j, k):
        there = chip_to(*OTHERS[k])
        return remote(
            part.at[ph, there, tiles(j)], got.at[ph, k, tiles(j)],
            rs_s.at[ph, j, k], rs_r.at[ph, j, k], {"chol": there * 2 + core},
        )

    def rs_start(ph, j):
        for k in range(7):
            rs_copy(ph, j, k).start()

    def rs_fin(ph, j):
        for k in range(7):
            rs_copy(ph, j, k).wait_recv()
        total = part[ph, chip, tiles(j)].astype(f32)
        for k in range(7):
            total = total + got[ph, k, tiles(j)].astype(f32)
        return total

    def matmul(ph, xg, j):
        start, size = SPANS[j]
        both = jnp.concatenate(
            [xg[start + n].reshape(1024, 128) for n in range(size)], axis=1
        )
        columns = pl.ds(0, 128 * size)
        for g in range(4):
            product = jnp.dot(
                lst[g].reshape(512, 1024), both, preferred_element_type=f32
            )
            scale = jnp.concatenate(
                [fb[g, pl.ds(start + n, 1), :] for n in range(size)], axis=1
            )
            if g == 0:
                acc[:, columns] = product * scale
            else:
                acc[:, columns] += product * scale
        for q in range(8):
            for n in range(size):
                part[ph, q, start + n] = acc[
                    pl.ds(64 * q, 64), pl.ds(128 * n, 128)
                ].astype(bf16)

    l_copy.start()

    @pl.loop(1, WALK)
    def _(d):
        s_copy(d, False).wait_recv()

    low = jnp.sum(
        jnp.where((lane8 == row8)[None], sall[...], 0.0), axis=2, keepdims=True
    )
    low = jnp.broadcast_to(low, (WALK, 8, 128))
    wanted = jnp.stack([low, low + 8], axis=1).reshape(WALK * 16, 128)
    wide = lax.broadcasted_iota(jnp.int32, (WALK * 16, 128), 1).astype(f32)
    picks = [jnp.where(wanted == wide + 128 * b, 1.0, 0.0).astype(bf16) for b in range(4)]

    @pl.loop(1, WALK)
    def _(d):
        z_copy(d, False).wait_recv()

    here = zrecv[...].reshape(WALK * 16, 128)
    taken = jnp.dot(picks[0], here[0:128], preferred_element_type=f32)
    for b in range(1, 4):
        taken = taken + jnp.dot(
            picks[b], here[128 * b : 128 * (b + 1)], preferred_element_type=f32
        )
    ysend[...] = taken.astype(bf16).reshape(WALK, 16, 128)
    yrecv[walk] = ysend[walk]

    @pl.loop(1, WALK)
    def _(d):
        y_copy(d, True).start()

    for load in loads[3:]:
        load.wait()
    own_h.wait()
    g_got.wait_recv()
    for k in range(7):
        hr_got(k).wait_recv()

    same = (
        lax.broadcasted_iota(jnp.int32, (64, 128), 0)
        == lax.broadcasted_iota(jnp.int32, (64, 128), 1) % 64
    ).astype(f32)

    def one_source(source, tile):
        pair = (hrg[source, 0], hrg[source, 1])
        picked = jnp.zeros((8, 128), f32)
        for half in range(2):
            columns = jnp.concatenate([h[:, 64 * half : 64 * half + 64] for h in pair], axis=1)
            product = jnp.dot(
                gp[:, half].reshape(512, 128), columns, preferred_element_type=f32
            )
            picked = picked + jnp.sum(product.reshape(8, 64, 128) * same[None], axis=1)
        for which in range(2):
            value = jnp.sum(
                jnp.where((lane8 >= 64) == bool(which), picked, 0.0), axis=1, keepdims=True
            )
            tile = jnp.where(
                lane8 == source * 4 + core * 2 + which, field_scale * value, tile
            )
        return tile

    tile = lax.fori_loop(0, 8, one_source, jnp.zeros((8, 128), f32))
    for which in range(2):
        shift = mean_in[index_in[which]]
        for w in range(8):
            tile = tile + jnp.where(
                (row8 == w) & (lane8 == chol * 2 + which),
                noise_in[which, w] - field_scale * shift, 0.0,
            )
    btile[chol] = tile

    def b_copy(d, sending):
        there = (chol + d) % 16 if sending else (chol + 16 - d) % 16
        slot = chol if sending else there
        return remote(
            btile.at[slot], btile.at[slot], b_s.at[d], b_r.at[d], {"chol": there}
        )

    @pl.loop(1, 16)
    def _(d):
        b_copy(d, True).start()

    @pl.loop(1, WALK)
    def _(d):
        y_copy(d, False).wait_recv()

    for p in range(WALK):
        both = yrecv[p].astype(f32)
        final[pl.ds(2 * p, 8, stride=64), :] = both[0:8]
        final[pl.ds(2 * p + 1, 8, stride=64), :] = both[8:16]
    lanes = lax.broadcasted_iota(jnp.int32, (64, 128), 1)
    shifted = [final[pl.ds(64 * w, 64)] for w in range(8)]
    shifted = [
        pltpu.roll(v, (OCC * w) % 128, 1) if w else v for w, v in enumerate(shifted)
    ]
    for t in range(TILES):
        tile = jnp.zeros((64, 128), f32)
        for w in range(8):
            left, right = OCC * w - 128 * t, OCC * (w + 1) - 128 * t
            if right > 0 and left < 128:
                tile = jnp.where((lanes >= left) & (lanes < right), shifted[w], tile)
        xg1[t, chol] = tile.astype(bf16)
    ag_start(0, xg1, 0)
    ag_start(0, xg1, 1)

    @pl.loop(1, 16)
    def _(d):
        b_copy(d, False).wait_recv()

    field = btile[0]
    for c in range(1, 16):
        field = field + btile[c]
    fall[pl.ds(pl.multiple_of(8 * walk, 8), 8)] = field

    @pl.loop(1, WALK)
    def _(d):
        f_copy(d, True).start()

    ag_relay(0, xg1, 0)
    ag_start(0, xg1, 2)

    @pl.loop(1, WALK)
    def _(d):
        f_copy(d, False).wait_recv()

    for s in range(8):
        fsel[pl.ds(s, 1), :] = fall[pl.ds(source_in[s], 1), :]
    field = fsel[...]
    for g in range(4):
        value = jnp.sum(
            jnp.where(lane8 == chip * 4 + g, field, 0.0), axis=1, keepdims=True
        )
        for t in range(TILES):
            column = lane8 + 128 * t
            mine = (column >= OCC * row8) & (column < OCC * (row8 + 1))
            fb[g, pl.ds(t, 1), :] = jnp.sum(
                jnp.where(mine, value, 0.0), axis=0, keepdims=True
            )

    ag_relay(0, xg1, 1)
    ag_start(0, xg1, 3)
    own_l.wait()
    l_got.wait_recv()

    def mm1(j):
        ag_fin(0, xg1, j)
        matmul(0, xg1, j)
        rs_start(0, j)

    def turn(j):
        term = field_scale * rs_fin(0, j)
        first[tiles(j)] = term
        xg2[tiles(j), chol] = term.astype(bf16)
        ag_start(1, xg2, j)

    def mm2(j):
        ag_fin(1, xg2, j)
        matmul(1, xg2, j)
        rs_start(1, j)

    def finish(j):
        done_tiles = (
            xg1[tiles(j), chol].astype(f32)
            + first[tiles(j)]
            + (0.5 * field_scale) * rs_fin(1, j)
        )
        first[tiles(j)] = done_tiles

    mm1(0)
    ag_relay(0, xg1, 2)
    mm1(1)
    ag_relay(0, xg1, 3)
    turn(0)
    mm1(2)
    turn(1)
    mm1(3)
    ag_relay(1, xg2, 0)
    turn(2)
    ag_relay(1, xg2, 1)
    mm2(0)
    turn(3)
    ag_relay(1, xg2, 2)
    mm2(1)
    ag_relay(1, xg2, 3)
    finish(0)
    mm2(2)
    finish(1)
    mm2(3)
    def unpack(w):
        t, start = (OCC * w) // 128, (OCC * w) % 128
        if start:
            mixed = jnp.where(lanes >= start, first[t], first[min(t + 1, TILES - 1)])
            mixed = pltpu.roll(mixed, 128 - start, 1)
        else:
            mixed = first[t]
        out_ref[w] = mixed[:, 0:OCC].astype(bf16)

    late = ((1, CHUNKS - 2), (1, CHUNKS - 1))
    g_copy.wait_send()
    l_copy.wait_send()
    for k in range(7):
        hr_copy(k).wait_send()

    @pl.loop(1, 16)
    def _(d):
        b_copy(d, True).wait_send()

    for ph, xg in ((0, xg1), (1, xg2)):
        for j in range(CHUNKS):
            for k in range(7):
                ag_send(ph, xg, j, k).wait_send()
                if (ph, j) not in late:
                    rs_copy(ph, j, k).wait_send()
            for k in range(8):
                sib(ph, xg, j, k, core).wait_send()

    @pl.loop(1, WALK)
    def _(d):
        s_copy(d, True).wait_send()
        z_copy(d, True).wait_send()
        y_copy(d, True).wait_send()
        f_copy(d, True).wait_send()

    finish(2)
    for w in range(6):
        unpack(w)
    finish(3)
    for w in range(6, 8):
        unpack(w)
    for ph, j in late:
        for k in range(7):
            rs_copy(ph, j, k).wait_send()


def per_device(
    cholesky, half_rotated, green_half, walker, aux_noise, mf_shift, chol_index, walker_source
):
    bf16, f32, i32 = jnp.bfloat16, jnp.float32, jnp.int32
    V, S, D = pltpu.VMEM, pltpu.SMEM, pltpu.SemaphoreType.DMA
    moved = pl.pallas_call(
        body,
        out_shape=jax.ShapeDtypeStruct((8, 64, OCC), bf16),
        in_specs=[pl.BlockSpec(memory_space=pltpu.HBM)] * 8,
        out_specs=pl.BlockSpec(memory_space=pltpu.VMEM),
        scratch_shapes=[
            V((4, 8, 64, 1024), bf16),
            V((TILES, 16, 64, 128), bf16),
            V((TILES, 16, 64, 128), bf16),
            V((2, 8, TILES, 64, 128), bf16),
            V((2, 7, TILES, 64, 128), bf16),
            V((TILES, 64, 128), f32),
            V((512, 256), f32),
            V((8, 2, 128, 128), bf16),
            V((8, 2, 64, 128), bf16),
            V((4, 8, 128), f32),
            V((16, 8, 128), f32),
            V((512, 128), f32),
            V((WALK, 16, 128), bf16),
            V((WALK, 16, 128), bf16),
            V((WALK, 16, 128), bf16),
            V((WALK, 16, 128), bf16),
            V((1, 128), f32),
            V((WALK, 1, 128), f32),
            V((256, 128), f32),
            V((8, 128), f32),
            V((8, 64, OCC), bf16),
            V((8, 64, OCC), bf16),
            S((2, 8), f32),
            S((4000,), f32),
            S((2,), i32),
            S((8,), i32),
            D((2, CHUNKS, 7)),
            D((2, CHUNKS, 7)),
            D((2, CHUNKS, 8)),
            D((2, CHUNKS, 8)),
            D((2, CHUNKS, 7)),
            D((2, CHUNKS, 7)),
            D((7,)),
            D((7,)),
            D((16,)),
            D((16,)),
            D((WALK,)),
            D((WALK,)),
            D((WALK,)),
            D((WALK,)),
            D((WALK,)),
            D((WALK,)),
            D((WALK,)),
            D((WALK,)),
            D((6,)),
            D((6,)),
        ],
        compiler_params=pltpu.CompilerParams(
            collective_id=0, has_side_effects=True, vmem_limit_bytes=64 * 1024 * 1024
        ),
        cost_estimate=pl.CostEstimate(
            flops=8_600_000_000, bytes_accessed=6_000_000, transcendentals=0
        ),
    )(
        cholesky.reshape(2, 8, 2, 64, 1024),
        jnp.pad(half_rotated, ((0, 0), (0, 12), (0, 0))),
        jnp.transpose(green_half, (0, 2, 1)),
        jnp.transpose(walker, (0, 2, 1)),
        jnp.transpose(aux_noise, (1, 0)),
        mf_shift,
        chol_index,
        walker_source,
    )
    return jnp.transpose(moved, (0, 2, 1))


def solution(mesh):
    placed = (
        P("chol", None, None),
        P("chol", None, None),
        P("walk", None, "chol"),
        P("walk", None, "chol"),
        P("walk", "chol"),
        P(),
        P("chol"),
        P("walk"),
    )
    return jax.shard_map(
        per_device, mesh=mesh, in_specs=placed, out_specs=P("walk", None, "chol"), check_vma=False
    )
```
